256 devices in a mesh: dp: 64 (over z, y, core), replica: 4 (over x).
Axes of the slice: x: 4, y: 4, z: 8, core: 2. Of those that a mesh axis runs over, the one named last changes fastest.
Arguments:
- text_features: bfloat16 [256, 4, 64, 4096], P('dp', 'replica'), may hold values from -6 to 6
- head_weight: bfloat16 [4096, 1024], replicated, may hold values from -0.09375 to 0.09375
- image_embeds: bfloat16 [256, 256, 1024], P('dp'), may hold values from -6 to 6
- doc_ids: int32 [256, 256], P('dp'), may hold values from 0 to 63, never falling along the last dimension, each value on 1 to 8 neighbouring positions
- hard_lists: int32 [256, 63], replicated, may hold values from -1 to 255, as said below
- logit_scale: float32 [], replicated, may hold values from 20 to 40
- logit_bias: float32 [], replicated, may hold values from -4 to -2
Outputs:
- row_loss: float32 [256, 256], P('dp', 'replica')
- head_grad: float32 [4096, 1024], P('replica', 'dp')
The draws below stay inside these ranges and needn't reach their ends.
Inputs may be any that keep to these rules, and one draw needn't show every extreme that they name: `hard_lists`: each row lists its text blocks first and -1 after them. The image blocks d * 4 to d * 4 + 3 together name at most one text block of each other dp index and none of blocks d * 4 to d * 4 + 3; some dp index names a block of every other dp index. `doc_ids`: within a row, ids never fall.
All inputs are finite; a program needn't handle non-finite values.
Results may differ from the reference program's by a relative error of at most 0.012.
Values may be sent and summed in bfloat16 or wider, within the bound.
No kernel may reach another device: no remote copies, remote signals or barrier semaphores. Data moves between devices by JAX's collectives and lax.ppermute only.
A program may use at most 128 MiB of HBM per device.

```python
import math
import jax
import jax.numpy as jnp
import numpy as np
from jax import lax

FEAT = 4096
EMB = 1024
BLK = 256
NBLK = 4
QROWS = 64
BLOCKS = 256
KMAX = 63
DOCS = 64
DOC_MOST = 8
N_DP = 64
N_REPLICA = 4


def draw_hard_lists(key, part):
    keys = jax.random.split(key, 5)
    dp_ids = jnp.arange(N_DP, dtype=jnp.int32)
    offsets = jax.vmap(lambda sub: jax.random.permutation(sub, N_DP - 1))(jax.random.split(keys[0], N_DP)) + 1
    peers = (dp_ids[:, None] + offsets.astype(jnp.int32)) % N_DP
    level = jax.random.randint(keys[1], (N_DP,), 0, 16)
    busiest = jax.random.randint(keys[2], (), 0, N_DP - 1)
    level = jnp.where(dp_ids == busiest, 15, level)
    request_count = 1 + (N_DP - 2) * level * level // 225
    slot_iota = jnp.arange(N_DP - 1, dtype=jnp.int32)
    valid = slot_iota[None, :] < request_count[:, None]
    image_block = jax.random.randint(keys[3], (N_DP, N_DP - 1), 0, NBLK)
    local_text = jax.random.randint(keys[4], (N_DP, N_DP - 1), 0, NBLK)
    forced = (dp_ids[:, None] == busiest) & (peers == N_DP - 1)
    local_text = jnp.where(forced, NBLK - 1, local_text)
    text_id = peers * NBLK + local_text
    onehot = ((image_block[..., None] == jnp.arange(NBLK, dtype=jnp.int32)) & valid[..., None]).astype(jnp.int32)
    position = jnp.sum(jnp.cumsum(onehot, axis=1) * onehot, axis=2) - 1
    position = jnp.where(valid, position, KMAX)
    target_row = dp_ids[:, None] * NBLK + image_block
    lists = jnp.full((BLOCKS, KMAX), -1, jnp.int32)
    return lists.at[target_row, position].set(text_id.astype(jnp.int32), mode='drop')


def levels(own_key, dims, shards, least, high):
    level, own = 1.0, jax.random.fold_in(own_key, 6)
    for dim, parts in shards:
        draws = jnp.exp(jax.random.uniform(jax.random.fold_in(own, dim), (parts,), jnp.float32, least / len(shards), high / len(shards)))
        level = level * jnp.repeat(draws, dims[dim] // parts).reshape([-1 if axis == dim else 1 for axis in range(len(dims))])
    return level


def profile(count, total, bound, slope):
    loads = [(1 << 20) // math.isqrt(rank ** slope) + 1 for rank in range(2, count + 1)]
    spare, counts = total - bound - (count - 1), [1] * (count - 1)
    while spare > 0:
        candidates = [i for i in range(count - 1) if counts[i] < bound]
        pool, budget = sum([loads[i] for i in candidates]), spare
        for i in candidates:
            extra = min(bound - counts[i], max(1, budget * loads[i] // pool), spare)
            counts[i] = counts[i] + extra
            spare = spare - extra
    return np.array([bound] + counts)


def uneven_parts(own_key, count, total, limit, slope):
    if count == 2:
        one = jax.random.randint(own_key, (), max(1, total - limit), min(limit, total - 1) + 1)
        return jnp.stack([one, total - one])
    sizes = jnp.asarray(profile(count, total, limit, slope), jnp.int32)
    pairs = (count - 1) // 2
    source_of, receiver = sizes[1:1 + 2 * pairs:2], sizes[2:2 + 2 * pairs:2]
    room = jnp.minimum(source_of - 1, limit - receiver)
    shifted = jax.random.randint(jax.random.fold_in(own_key, 1), (pairs,), 0, 1 << 20) % (room + 1)
    sizes = sizes.at[1:1 + 2 * pairs:2].set(source_of - shifted).at[2:2 + 2 * pairs:2].set(receiver + shifted)
    return sizes[jax.random.permutation(jax.random.fold_in(own_key, 2), count)]


def noise(key, shape, spread, bound, cuts=(), held_as=jnp.bfloat16):
    values = jax.random.normal(key, shape, jnp.float32) * spread
    if len(cuts) > 0:
        values = levels(key, shape, cuts, -0.22, 0.18) * values
    return jnp.clip(values, min=-bound, max=bound).astype(held_as)


def setup_inputs(seed: int = 0) -> dict:
    key_list = jax.random.split(jax.random.key(seed), 8)
    text_features = noise(key_list[0], (BLOCKS, N_REPLICA, QROWS, FEAT), 1.0, 6.0, ((0, 64), (1, 4)))
    head_weight = noise(key_list[1], (FEAT, EMB), FEAT ** -0.5, 0.09375)
    image_embeds = noise(key_list[2], (BLOCKS, BLK, EMB), 1.0, 6.0, ((0, 64),))
    doc_ids = jax.vmap(lambda own: jnp.searchsorted(jnp.cumsum(uneven_parts(own, DOCS, BLK, DOC_MOST, 0)), jnp.arange(BLK), side="right"))(jax.random.split(key_list[3], BLOCKS)).reshape((BLOCKS, BLK)).astype(jnp.int32)
    hard_lists = draw_hard_lists(jax.random.fold_in(key_list[7], 71), 0)
    logit_scale = jnp.clip(jax.random.uniform(key_list[5], (), jnp.float32, 20.0, 40.0), 20.0, 40.0)
    logit_bias = jnp.clip(jax.random.uniform(key_list[6], (), jnp.float32, -4.0, -2.0), -4.0, -2.0)
    return {"text_features": text_features, "head_weight": head_weight, "image_embeds": image_embeds, "doc_ids": doc_ids, "hard_lists": hard_lists, "logit_scale": logit_scale, "logit_bias": logit_bias}


EPSILON = 1e-06

def unit_rows(values):
    inverse = lax.rsqrt(lax.optimization_barrier(jnp.sum(values * values, axis=-1, keepdims=True)) + EPSILON)
    return (values * inverse, inverse)

def reference(text_features, head_weight, image_embeds, doc_ids, hard_lists, logit_scale, logit_bias):
    text_rows = text_features.reshape(BLOCKS * BLK, FEAT)
    projected = jnp.dot(text_rows, head_weight, preferred_element_type=jnp.float32)
    unit_text, inverse = unit_rows(projected)
    unit_text = unit_text.reshape(BLOCKS, BLK, EMB)
    inverse = inverse.reshape(BLOCKS, BLK, 1)
    text_emb = unit_text.astype(jnp.bfloat16)
    image_unit = unit_rows(image_embeds.astype(jnp.float32))[0].astype(jnp.bfloat16)

    def own_block(inputs):
        image_block, text_block, doc_row = inputs
        logits = logit_scale * jnp.dot(image_block, text_block.T, preferred_element_type=jnp.float32) + logit_bias
        label_sign = jnp.where(doc_row[:, None] == doc_row[None, :], 1.0, -1.0).astype(jnp.float32)
        elem_loss = jax.nn.softplus(-label_sign * logits)
        weights = (-label_sign * jax.nn.sigmoid(-label_sign * logits)).astype(jnp.bfloat16)
        text_grads = logit_scale * jnp.dot(weights.T, image_block, preferred_element_type=jnp.float32)
        return (lax.optimization_barrier(jnp.sum(elem_loss, axis=1)), text_grads)
    own_loss, own_grad = lax.map(own_block, (image_unit, text_emb, doc_ids))
    flat_lists = hard_lists.reshape(-1).astype(jnp.int32)
    live_flag = (flat_lists >= 0).astype(jnp.int32)
    pair_order = jnp.argsort(1 - live_flag, stable=True).astype(jnp.int32)
    live_total = jnp.sum(live_flag).astype(jnp.int32)

    def visit(step_index, carry):
        loss_acc, grad_acc = carry
        pair_index = pair_order[step_index]
        image_index = (pair_index // KMAX).astype(jnp.int32)
        text_index = flat_lists[pair_index].astype(jnp.int32)
        image_block = lax.dynamic_index_in_dim(image_unit, image_index, 0, keepdims=False)
        text_block = lax.dynamic_index_in_dim(text_emb, text_index, 0, keepdims=False)
        logits = logit_scale * jnp.dot(image_block, text_block.T, preferred_element_type=jnp.float32) + logit_bias
        weights = jax.nn.sigmoid(logits).astype(jnp.bfloat16)
        part_grad = (logit_scale * jnp.dot(weights.T, image_block, preferred_element_type=jnp.float32)).astype(jnp.bfloat16)
        part_grad = lax.optimization_barrier(part_grad).astype(jnp.float32)
        loss_acc = loss_acc.at[image_index].add(lax.optimization_barrier(jnp.sum(jax.nn.softplus(logits), axis=1)))
        grad_acc = grad_acc.at[text_index].add(part_grad)
        return (loss_acc, grad_acc)
    start_carry = (jnp.zeros((BLOCKS, BLK), jnp.float32), jnp.zeros((BLOCKS, BLK, EMB), jnp.float32))
    remote_loss, remote_grad = lax.fori_loop(jnp.int32(0), live_total, visit, start_carry)
    row_loss = (own_loss + remote_loss) / BLK
    text_grad = own_grad + remote_grad
    along = lax.optimization_barrier(jnp.sum(unit_text * text_grad, axis=-1, keepdims=True))
    proj_grad = ((text_grad - unit_text * along) * inverse).astype(jnp.bfloat16)
    feat_blocks = text_features.reshape(N_DP, NBLK, N_REPLICA, QROWS, FEAT)
    grad_blocks = proj_grad.reshape(N_DP, NBLK, N_REPLICA, QROWS, EMB)

    def add_device(grad_sum, dp_index):
        feat_rows = lax.dynamic_index_in_dim(feat_blocks, dp_index, 0, keepdims=False).astype(jnp.float32)
        grad_rows = lax.dynamic_index_in_dim(grad_blocks, dp_index, 0, keepdims=False).astype(jnp.float32)
        dev_terms = jnp.einsum('brqf,brqe->rfe', feat_rows, grad_rows)
        rounded = lax.optimization_barrier(dev_terms.astype(jnp.bfloat16)).astype(jnp.float32)
        return (grad_sum + lax.optimization_barrier(jnp.sum(rounded, axis=0)), None)
    head_grad = lax.scan(add_device, jnp.zeros((FEAT, EMB), jnp.float32), jnp.arange(N_DP, dtype=jnp.int32))[0]
    return (row_loss, head_grad)
```

```python
import functools

import jax
import jax.numpy as jnp
from jax import lax
from jax.experimental import pallas as pl
from jax.experimental.pallas import tpu as pltpu
from jax.sharding import Mesh, PartitionSpec as P

EPSILON = 1e-06
DP = ("z", "y", "c")
GROUP = 4
F32 = jnp.float32
BF16 = jnp.bfloat16


def dot(a, b, contract):
    return lax.dot_general(a, b, ((contract[:1], contract[1:]), ((), ())), preferred_element_type=F32)


def unit_rows(values):
    inverse = lax.rsqrt(jnp.sum(values * values, axis=-1, keepdims=True) + EPSILON)
    return (values * inverse, inverse)


def shifted(size, shift):
    return [(i, (i + shift) % size) for i in range(size)]


def loss_and_weight(logits):
    small = jnp.exp(-jnp.abs(logits))
    share = 1.0 / (1.0 + small)
    weight = jnp.where(logits >= 0, share, small * share)
    return (jnp.maximum(logits, 0.0) + jnp.log1p(small), weight)


def pair_kernel(
    sources, counts, place, scale_bias, text_0, text_1, text_2, text_3, inverse, own_images,
    image_docs, text_docs, arrived, chunks, pair_loss, own_loss, text_all, acc
):
    blocks, piece_rows, width = text_0.shape
    pieces = (text_0, text_1, text_2, text_3)
    quarters = len(pieces)
    block_rows = quarters * piece_rows
    part = width // quarters
    scale, bias = scale_bias[0], scale_bias[1]
    for k in range(quarters):
        text_all[:, k * piece_rows : (k + 1) * piece_rows, :] = pieces[k][...]
    pair_loss[...] = jnp.zeros_like(pair_loss)

    def each_block(t, carry):
        text = text_all[t]
        images = own_images[t]
        logits = scale * dot(text, images, (1, 1)) + bias
        same = text_docs[t] == image_docs[t]
        sign = jnp.where(same, 1.0, -1.0)
        loss, weight = loss_and_weight(-sign * logits)
        own_loss[pl.ds(t, 1)] = jnp.sum(loss, axis=0, keepdims=True)[None]
        acc[...] = dot((-sign * weight).astype(BF16), images, (1, 0))
        count = counts[t]

        def each_group(g, inner):
            ids = [sources[t, g * GROUP + i] for i in range(GROUP)]
            rows = jnp.concatenate([arrived[ids[i]] for i in range(GROUP)], axis=0)
            values = scale * dot(text, rows, (1, 1)) + bias
            terms, shares = loss_and_weight(values)
            sums = jnp.sum(terms, axis=0, keepdims=True)
            left = (count - g * GROUP) * piece_rows
            live = lax.broadcasted_iota(jnp.int32, shares.shape, 1) < left
            shares = jnp.where(live, shares, 0.0).astype(BF16)
            acc[...] += dot(shares, rows, (1, 0))
            for i in range(GROUP):

                @pl.when(g * GROUP + i < count)
                def _():
                    pair_loss[pl.ds(ids[i], 1)] = sums[:, i * piece_rows : (i + 1) * piece_rows][None]

            return inner

        lax.fori_loop(0, (count + GROUP - 1) // GROUP, each_group, 0)
        unit = text.astype(F32)
        grad = scale * acc[...]
        along = jnp.sum(unit * grad, axis=-1, keepdims=True)
        acc[...] = (grad - unit * along) * inverse[t]
        for k in range(quarters):
            start = pl.multiple_of(lax.rem(place[0] + k, quarters) * part, part)
            values = acc[:, pl.ds(start, part)].astype(BF16)
            for j in range(quarters):
                chunks[k, j, pl.ds(t, 1)] = values[j * piece_rows : (j + 1) * piece_rows][None]
        return carry

    lax.fori_loop(0, blocks, each_block, 0)


def head_kernel(
    place, grad_0, grad_1, grad_2, grad_3, feat_0, feat_1, feat_2, feat_3, keep, give, turned,
    *, sizes, strip
):
    z_part, y_size, c_size = sizes
    feats = (feat_0, feat_1, feat_2, feat_3)
    rows = feat_0.shape[0]

    @pl.when(pl.program_id(0) == 0)
    def _():
        for j in range(len(feats)):
            at = slice(j * rows, (j + 1) * rows)
            total = 0.0
            for k, grad in enumerate((grad_0, grad_1, grad_2, grad_3)):
                piece = (j - k) % len(feats)
                total += grad[piece * rows : (piece + 1) * rows].astype(F32)
            flipped = total.T.astype(BF16)
            for zz in range(z_part):
                for y in range(y_size):
                    for c in range(c_size):
                        block = flipped[((zz * y_size + y) * c_size + c) * strip :][:strip]
                        y_rel = lax.rem(y - place[1] + y_size, y_size)
                        c_rel = lax.rem(c - place[2] + c_size, c_size)
                        to = ((c_rel * y_size + y_rel) * z_part + zz) * strip
                        turned[pl.ds(pl.multiple_of(to, strip), strip), at] = block

    half = keep.shape[0]
    for part, out in enumerate((keep, give)):
        total = None
        for j, feat in enumerate(feats):
            term = dot(turned[part * half : (part + 1) * half, j * rows : (j + 1) * rows], feat[...], (1, 0))
            total = term if total is None else total + term
        out[...] = total.astype(BF16)


def whole(memory=pltpu.VMEM):
    return pl.BlockSpec(memory_space=memory)


def on_device(
    text_features, head_weight, image_embeds, doc_ids, hard_lists, logit_scale, logit_bias
):
    z_size, y_size, c_size, x_size = (lax.axis_size(name) for name in ("z", "y", "c", "x"))
    z, y, c, x = (lax.axis_index(name) for name in ("z", "y", "c", "x"))
    dp_count = z_size * y_size * c_size
    dp_index = (z * y_size + y) * c_size + c
    blocks, _, piece_rows, feat_width = text_features.shape
    block_rows = image_embeds.shape[1]
    emb_width = head_weight.shape[1]
    rows = blocks * piece_rows
    part = emb_width // x_size
    strip = emb_width // dp_count
    block_iota = jnp.arange(blocks, dtype=jnp.int32)
    peer_iota = jnp.arange(dp_count, dtype=jnp.int32)

    owners = jnp.where(hard_lists >= 0, hard_lists // blocks, -1).reshape(dp_count, blocks, -1)
    my_owners = lax.dynamic_index_in_dim(owners, dp_index, 0, keepdims=False)
    asked = jnp.any(my_owners[None] == peer_iota[:, None, None], axis=2)
    asker_block = jnp.sum(asked.astype(jnp.int32) * block_iota, axis=1)

    own_images = lax.dynamic_slice_in_dim(image_embeds, x * piece_rows, piece_rows, 1)
    own_images = unit_rows(own_images.astype(F32))[0].astype(BF16)
    arrived = exchange_images(own_images, asker_block)

    features = text_features.reshape(rows, feat_width)
    unit_text, inverse = unit_rows(dot(features, head_weight, (1, 0)))
    text_emb = unit_text.astype(BF16).reshape(blocks, piece_rows, emb_width)
    inverse = inverse.reshape(blocks, piece_rows)

    def around(value):
        return [value] + [lax.ppermute(value, "x", shifted(x_size, k)) for k in range(1, x_size)]

    texts = around(text_emb)
    inverses = jnp.stack(around(inverse), axis=1).reshape(blocks, block_rows, 1)
    feats = around(features)

    hit = (owners == dp_index)
    listed = jnp.any(hit, axis=(1, 2))
    which = jnp.sum(hit * (hard_lists % blocks).reshape(owners.shape), axis=(1, 2))
    mine = listed[None] & (which[None] == block_iota[:, None])
    before = peer_iota[None] < peer_iota[:, None]
    order = jnp.sum((mine[:, None] & before).astype(jnp.int32), axis=2)
    counts = jnp.sum(mine.astype(jnp.int32), axis=1)
    slots = jnp.arange(dp_count, dtype=jnp.int32)
    sources = jnp.sum(
        jnp.where(mine[:, None] & (order[:, None] == slots[:, None]), peer_iota, 0), axis=2
    )

    docs = doc_ids.reshape(blocks, x_size, piece_rows)
    twice = jnp.concatenate([docs[:, ::-1], docs[:, ::-1]], axis=1)
    text_docs = lax.dynamic_slice_in_dim(twice, x_size - 1 - x, x_size, 1)
    text_docs = text_docs.reshape(blocks, block_rows, 1)
    image_docs = lax.dynamic_index_in_dim(docs, x, 1, keepdims=True)
    place = jnp.stack([x, y, c]).astype(jnp.int32)
    scale_bias = jnp.stack([logit_scale, logit_bias])

    chunks, pair_loss, own_loss = pl.pallas_call(
        pair_kernel,
        out_shape=(
            jax.ShapeDtypeStruct((x_size, x_size, blocks, piece_rows, part), BF16),
            jax.ShapeDtypeStruct((dp_count, 1, piece_rows), F32),
            jax.ShapeDtypeStruct((blocks, 1, piece_rows), F32),
        ),
        in_specs=[whole(pltpu.SMEM)] * 4 + [whole()] * 9,
        out_specs=(whole(), whole(), whole()),
        scratch_shapes=[
            pltpu.VMEM((blocks, block_rows, emb_width), BF16),
            pltpu.VMEM((block_rows, emb_width), F32),
        ],
        compiler_params=pltpu.CompilerParams(vmem_limit_bytes=48 << 20),
        name="pairs",
    )(sources, counts, place, scale_bias, *texts, inverses, own_images, image_docs, text_docs, arrived)

    returned = lax.all_to_all(
        pair_loss.reshape(dp_count, piece_rows), DP, split_axis=0, concat_axis=0, tiled=True
    )
    pick = (jnp.any(asked, axis=1)[:, None] & (asker_block[:, None] == block_iota))[..., None]
    remote_loss = jnp.sum(jnp.where(pick, returned[:, None], 0.0), axis=0)
    row_loss = (own_loss.reshape(blocks, piece_rows) + remote_loss) / block_rows

    grads = [chunks[0].reshape(x_size * rows, part)]
    for k in range(1, x_size):
        grads.append(
            lax.ppermute(chunks[k].reshape(x_size * rows, part), "x", shifted(x_size, k))
        )
    z_part = z_size // x_size
    tile = min(1024, feat_width)
    half = part // c_size
    keep, give = pl.pallas_call(
        functools.partial(head_kernel, sizes=(z_part, y_size, c_size), strip=strip),
        grid=(feat_width // tile,),
        out_shape=(
            jax.ShapeDtypeStruct((half, feat_width), BF16),
            jax.ShapeDtypeStruct((half, feat_width), BF16),
        ),
        in_specs=[whole(pltpu.SMEM)]
        + [whole()] * 4
        + [pl.BlockSpec((rows, tile), lambda i: (0, i))] * 4,
        out_specs=(
            pl.BlockSpec((half, tile), lambda i: (0, i)),
            pl.BlockSpec((half, tile), lambda i: (0, i)),
        ),
        scratch_shapes=[pltpu.VMEM((part, x_size * rows), BF16)],
        compiler_params=pltpu.CompilerParams(vmem_limit_bytes=48 << 20),
        name="head",
    )(place, *grads, *feats)

    taken = lax.ppermute(give, "c", shifted(c_size, 1))
    total = (keep.astype(F32) + taken.astype(F32)).astype(BF16)
    total = total.reshape(y_size, z_part * strip, feat_width)
    moved = [total[0]] + [
        lax.ppermute(total[k], "y", shifted(y_size, k)) for k in range(1, y_size)
    ]
    total = sum(m.astype(F32) for m in moved).astype(BF16)
    total = total.reshape(z_part, strip, x_size, feat_width // x_size)
    final = None
    for k in range(z_size):
        goes = lax.rem(z + k, z_size)
        chunk = lax.dynamic_slice(
            total, (goes // x_size, 0, goes % x_size, 0), (1, strip, 1, feat_width // x_size)
        ).reshape(strip, feat_width // x_size)
        pairs = []
        for z_from in range(z_size):
            for x_from in range(x_size):
                to = (z_from + k) % z_size
                pairs.append(
                    (z_from * x_size + x_from, (z_part * x_from + to // x_size) * x_size + to % x_size)
                )
        got = lax.ppermute(chunk, ("z", "x"), pairs).astype(F32)
        final = got if final is None else final + got
    return (row_loss, final.T)


def copy_kernel(picked, from_ref, to_ref):
    to_ref[...] = from_ref[...]


def pick_blocks(values, picked):
    count, shape = picked.shape[0], values.shape[1:]
    spec = pltpu.PrefetchScalarGridSpec(
        num_scalar_prefetch=1,
        grid=(count,),
        in_specs=[pl.BlockSpec((1,) + shape, lambda i, ref: (ref[i], 0, 0))],
        out_specs=pl.BlockSpec((1,) + shape, lambda i, ref: (i, 0, 0)),
    )
    return pl.pallas_call(
        copy_kernel,
        grid_spec=spec,
        out_shape=jax.ShapeDtypeStruct((count,) + shape, values.dtype),
        name="pick",
    )(picked, values)


def exchange_images(own_images, asker_block):
    outgoing = pick_blocks(own_images, asker_block)
    return lax.all_to_all(outgoing, DP, split_axis=0, concat_axis=0, tiled=True)


def solution(mesh):
    x_size = mesh.shape["replica"]
    c_size = 2
    z_size = 2 * x_size
    y_size = mesh.shape["dp"] // (z_size * c_size)
    fine = Mesh(mesh.devices.reshape(z_size, y_size, c_size, x_size), ("z", "y", "c", "x"))
    placed = (P(DP, "x", None, None), P(), P(DP, None, None), P(DP, None), P(), P(), P())
    return jax.shard_map(
        on_device,
        mesh=fine,
        in_specs=placed,
        out_specs=(P(DP, "x"), P("x", DP)),
        check_vma=False,
    )
```

```python
import functools

import jax
import jax.numpy as jnp
from jax import lax
from jax.experimental import pallas as pl
from jax.experimental.pallas import tpu as pltpu
from jax.sharding import Mesh, PartitionSpec as P

EPSILON = 1e-06
DP = ("z", "y", "c")
GROUP = 4
EXTRA = 128
F32 = jnp.float32
BF16 = jnp.bfloat16


def dot(a, b, contract):
    return lax.dot_general(a, b, ((contract[:1], contract[1:]), ((), ())), preferred_element_type=F32)


def unit_rows(values):
    inverse = lax.rsqrt(jnp.sum(values * values, axis=-1, keepdims=True) + EPSILON)
    return (values * inverse, inverse)


def shifted(size, shift):
    return [(i, (i + shift) % size) for i in range(size)]


def loss_and_weight(logits):
    small = jnp.exp(-jnp.abs(logits))
    share = 1.0 / (1.0 + small)
    weight = jnp.where(logits >= 0, share, small * share)
    return (jnp.maximum(logits, 0.0) + jnp.log1p(small), weight)


def project_kernel(features, weight, out, acc):
    step = pl.program_id(0)

    @pl.when(step == 0)
    def _():
        acc[...] = jnp.zeros_like(acc)

    acc[...] += dot(features[...], weight[...], (1, 0))

    @pl.when(step == pl.num_programs(0) - 1)
    def _():
        unit, inverse = unit_rows(acc[...])
        width = unit.shape[1]
        out[:, :width] = unit.astype(BF16)
        first = inverse.astype(BF16).astype(F32)
        second = (inverse - first).astype(BF16).astype(F32)
        third = inverse - first - second
        lane = lax.broadcasted_iota(jnp.int32, (unit.shape[0], EXTRA), 1)
        terms = jnp.where(lane == 0, first, jnp.where(lane == 1, second, jnp.where(lane == 2, third, 0.0)))
        out[:, width:] = terms.astype(BF16)


def pair_kernel(sources, slots, counts, place, scale_bias, *refs, starts):
    quarters = 4
    texts, refs = refs[:quarters], refs[quarters:]
    own_images, image_docs, text_docs, *arriving = refs[:-7]
    chunks, pair_loss, own_loss, text_all, arrived, acc, sems = refs[-7:]
    blocks, piece_rows, width = own_images.shape
    part = width // quarters
    scale, bias = scale_bias[0], scale_bias[1]
    copies = []
    for n, (ref, at) in enumerate(zip(arriving, starts)):
        copies.append(pltpu.make_async_copy(ref, arrived.at[pl.ds(at, ref.shape[0])], sems.at[n]))
        copies[-1].start()
    for k in range(quarters):
        to = pl.multiple_of(lax.rem(place[0] - k + quarters, quarters) * piece_rows, piece_rows)
        text_all[:, pl.ds(to, piece_rows), :] = texts[k][...].reshape(blocks, piece_rows, width + EXTRA)
    pair_loss[...] = jnp.zeros_like(pair_loss)
    for copy in copies:
        copy.wait()

    def each_block(t, carry):
        text = text_all[t, :, :width]
        images = own_images[t]
        logits = scale * dot(text, images, (1, 1)) + bias
        same = text_docs[t] == image_docs[t]
        sign = jnp.where(same, 1.0, -1.0)
        loss, weight = loss_and_weight(-sign * logits)
        own_loss[pl.ds(t, 1)] = jnp.sum(loss, axis=0, keepdims=True)[None]
        acc[...] = dot((-sign * weight).astype(BF16), images, (1, 0))
        count = counts[t]

        def each_group(g, inner):
            held = [slots[t, g * GROUP + i] for i in range(GROUP)]
            rows = jnp.concatenate([arrived[held[i]] for i in range(GROUP)], axis=0)
            values = scale * dot(text, rows, (1, 1)) + bias
            terms, shares = loss_and_weight(values)
            sums = jnp.sum(terms, axis=0, keepdims=True)
            left = (count - g * GROUP) * piece_rows
            live = lax.broadcasted_iota(jnp.int32, shares.shape, 1) < left
            shares = jnp.where(live, shares, 0.0).astype(BF16)
            acc[...] += dot(shares, rows, (1, 0))
            for i in range(GROUP):

                @pl.when(g * GROUP + i < count)
                def _():
                    source = sources[t, g * GROUP + i]
                    pair_loss[pl.ds(source, 1)] = sums[:, i * piece_rows : (i + 1) * piece_rows][None]

            return inner

        lax.fori_loop(0, (count + GROUP - 1) // GROUP, each_group, 0)
        inverse = jnp.sum(text_all[t, :, width:].astype(F32), axis=-1, keepdims=True)
        unit = text.astype(F32)
        grad = scale * acc[...]
        along = jnp.sum(unit * grad, axis=-1, keepdims=True)
        acc[...] = (grad - unit * along) * inverse
        for k in range(quarters):
            start = pl.multiple_of(lax.rem(place[0] + k, quarters) * part, part)
            values = acc[:, pl.ds(start, part)].astype(BF16)
            for j in range(quarters):
                chunks[k, j, pl.ds(t, 1)] = values[j * piece_rows : (j + 1) * piece_rows][None]
        return carry

    lax.fori_loop(0, blocks, each_block, 0)


def pick_kernel(table, place, *refs, steps, sizes):
    z_size, y_size, c_size = sizes
    count = len(steps)
    from_refs, to_refs, sems = refs[:count], refs[count:-1], refs[-1]
    copies = []
    for dy in range(y_size):
        for dc in range(c_size):
            y = lax.rem(place[1] + dy, y_size)
            c = lax.rem(place[2] + dc, c_size)
            for j, step in enumerate(steps):
                z = lax.rem(place[3] - step + z_size, z_size)
                block = table[z, y * c_size + c]
                n = dy * c_size + dc
                copies.append(
                    pltpu.make_async_copy(from_refs[j].at[block], to_refs[n].at[j], sems.at[n * count + j])
                )
    for copy in copies:
        copy.start()
    for copy in copies:
        copy.wait()


def head_kernel(place, grad_0, grad_1, grad_2, grad_3, feats, keep, give, turned, *, sizes, strip):
    z_part, y_size, c_size = sizes

    @pl.when(pl.program_id(0) == 0)
    def _():
        total = sum(g[...].astype(F32) for g in (grad_0, grad_1, grad_2, grad_3))
        flipped = total.T.astype(BF16)
        for zz in range(z_part):
            for y in range(y_size):
                for c in range(c_size):
                    block = flipped[((zz * y_size + y) * c_size + c) * strip :][:strip]
                    y_rel = lax.rem(y - place[1] + y_size, y_size)
                    c_rel = lax.rem(c - place[2] + c_size, c_size)
                    to = ((c_rel * y_size + y_rel) * z_part + zz) * strip
                    turned[pl.ds(pl.multiple_of(to, strip), strip)] = block

    half = keep.shape[0]
    total = dot(turned[...], feats[...], (1, 0)).astype(BF16)
    keep[...] = total[:half]
    give[...] = total[half:]


def whole(memory=pltpu.VMEM):
    return pl.BlockSpec(memory_space=memory)


def on_device(
    text_features, head_weight, image_embeds, doc_ids, hard_lists, logit_scale, logit_bias
):
    z_size, y_size, c_size, x_size = (lax.axis_size(name) for name in ("z", "y", "c", "x"))
    z, y, c, x = (lax.axis_index(name) for name in ("z", "y", "c", "x"))
    dp_count = z_size * y_size * c_size
    dp_index = (z * y_size + y) * c_size + c
    blocks, _, piece_rows, feat_width = text_features.shape
    block_rows = image_embeds.shape[1]
    emb_width = head_weight.shape[1]
    rows = blocks * piece_rows
    part = emb_width // x_size
    strip = emb_width // dp_count
    block_iota = jnp.arange(blocks, dtype=jnp.int32)
    peer_iota = jnp.arange(dp_count, dtype=jnp.int32)
    place = jnp.stack([x, y, c, z]).astype(jnp.int32)
    features = text_features.reshape(rows, feat_width)
    feats = lax.all_gather(features, "x", axis=0, tiled=False)

    owners = jnp.where(hard_lists >= 0, hard_lists // blocks, -1).reshape(dp_count, blocks, -1)
    line = owners.reshape(z_size, y_size * c_size, blocks, -1)
    line = lax.dynamic_index_in_dim(line, y * c_size + c, 1, keepdims=False)
    plane = z * y_size * c_size + jnp.arange(y_size * c_size, dtype=jnp.int32)
    wanted = jnp.any(line[:, None] == plane[:, None, None], axis=3)
    table = jnp.sum(wanted.astype(jnp.int32) * block_iota, axis=2)

    own_images = lax.dynamic_slice_in_dim(image_embeds, x * piece_rows, piece_rows, 1)
    own_images = unit_rows(own_images.astype(F32))[0].astype(BF16)
    groups = exchange_images(own_images, table, place, (z_size, y_size, c_size))

    tile = min(1024, feat_width)
    text_emb = pl.pallas_call(
        project_kernel,
        grid=(feat_width // tile,),
        out_shape=jax.ShapeDtypeStruct((rows, emb_width + EXTRA), BF16),
        in_specs=[
            pl.BlockSpec((rows, tile), lambda i: (0, i)),
            pl.BlockSpec((tile, emb_width), lambda i: (i, 0)),
        ],
        out_specs=pl.BlockSpec((rows, emb_width + EXTRA), lambda i: (0, 0)),
        scratch_shapes=[pltpu.VMEM((rows, emb_width), F32)],
        compiler_params=pltpu.CompilerParams(vmem_limit_bytes=32 << 20),
        cost_estimate=pl.CostEstimate(
            flops=2 * rows * feat_width * emb_width, bytes_accessed=12 << 20, transcendentals=0
        ),
        name="project",
    )(features, head_weight)
    texts = [text_emb] + [
        lax.ppermute(text_emb, "x", shifted(x_size, k)) for k in range(1, x_size)
    ]

    hit = owners == dp_index
    listed = jnp.any(hit, axis=(1, 2))
    which = jnp.sum(hit * (hard_lists % blocks).reshape(owners.shape), axis=(1, 2))
    mine = listed[None] & (which[None] == block_iota[:, None])
    before = peer_iota[None] < peer_iota[:, None]
    order = jnp.sum((mine[:, None] & before).astype(jnp.int32), axis=2)
    counts = jnp.sum(mine.astype(jnp.int32), axis=1)
    at = mine[:, None] & (order[:, None] == peer_iota[:, None])
    sources = jnp.sum(jnp.where(at, peer_iota, 0), axis=2)
    back = (z - peer_iota // (y_size * c_size)) % z_size
    turn = jnp.where(2 * back <= z_size, jnp.maximum(2 * back - 1, 0), 2 * (z_size - back))
    over_y = (y - peer_iota // c_size) % y_size
    over_c = (c - peer_iota) % c_size
    slots = jnp.sum(jnp.where(at, (over_y * c_size + over_c) * z_size + turn, 0), axis=2)

    text_docs = doc_ids.reshape(blocks, block_rows, 1)
    image_docs = lax.dynamic_slice_in_dim(doc_ids, x * piece_rows, piece_rows, 1)[:, None]
    scale_bias = jnp.stack([logit_scale, logit_bias])
    arriving, starts, turns = [], [], 0
    for group in groups:
        arriving += group
        starts += [n * z_size + turns for n in range(len(group))]
        turns += group[0].shape[0]

    chunks, pair_loss, own_loss = pl.pallas_call(
        functools.partial(pair_kernel, starts=starts),
        out_shape=(
            jax.ShapeDtypeStruct((x_size, x_size, blocks, piece_rows, part), BF16),
            jax.ShapeDtypeStruct((dp_count, 1, piece_rows), F32),
            jax.ShapeDtypeStruct((blocks, 1, piece_rows), F32),
        ),
        in_specs=[whole(pltpu.SMEM)] * 5 + [whole()] * 7 + [whole(pl.ANY)] * len(arriving),
        out_specs=(whole(), whole(), whole()),
        scratch_shapes=[
            pltpu.VMEM((blocks, block_rows, emb_width + EXTRA), BF16),
            pltpu.VMEM((dp_count, piece_rows, emb_width), BF16),
            pltpu.VMEM((block_rows, emb_width), F32),
            pltpu.SemaphoreType.DMA((len(arriving),)),
        ],
        compiler_params=pltpu.CompilerParams(vmem_limit_bytes=48 << 20),
        cost_estimate=pl.CostEstimate(flops=8 << 30, bytes_accessed=20 << 20, transcendentals=4 << 20),
        name="pairs",
    )(sources, slots, counts, place, scale_bias, *texts, own_images, image_docs, text_docs, *arriving)

    grads = [chunks[0].reshape(x_size * rows, part)]
    for k in range(1, x_size):
        grads.append(
            lax.ppermute(chunks[k].reshape(x_size * rows, part), "x", shifted(x_size, k))
        )
    z_part = z_size // x_size
    half = part // c_size
    keep, give = pl.pallas_call(
        functools.partial(head_kernel, sizes=(z_part, y_size, c_size), strip=strip),
        grid=(feat_width // tile,),
        out_shape=(
            jax.ShapeDtypeStruct((half, feat_width), BF16),
            jax.ShapeDtypeStruct((half, feat_width), BF16),
        ),
        in_specs=[whole(pltpu.SMEM)]
        + [whole()] * 4
        + [pl.BlockSpec((x_size * rows, tile), lambda i: (0, i))],
        out_specs=(
            pl.BlockSpec((half, tile), lambda i: (0, i)),
            pl.BlockSpec((half, tile), lambda i: (0, i)),
        ),
        scratch_shapes=[pltpu.VMEM((part, x_size * rows), BF16)],
        compiler_params=pltpu.CompilerParams(vmem_limit_bytes=48 << 20),
        cost_estimate=pl.CostEstimate(
            flops=2 * rows * feat_width * emb_width, bytes_accessed=16 << 20, transcendentals=0
        ),
        name="head",
    )(place, *grads, feats.reshape(x_size * rows, feat_width))

    asker = jnp.sum(jnp.any(hit, axis=2).astype(jnp.int32) * block_iota, axis=1)
    spread = jnp.where(asker[:, None, None] == block_iota[:, None], pair_loss, 0.0)
    remote_loss = lax.psum_scatter(spread.reshape(dp_count * blocks, piece_rows), DP, tiled=True)
    row_loss = (own_loss.reshape(blocks, piece_rows) + remote_loss) / block_rows
    return (row_loss, add_over_dp(keep, give, (z_size, y_size, c_size, x_size), z, strip))


def add_over_dp(keep, give, sizes, z, strip):
    z_size, y_size, c_size, x_size = sizes
    z_part = z_size // x_size
    width = keep.shape[1]

    def add(*values):
        return sum(v.astype(F32) for v in values).astype(BF16)

    total = add(keep, lax.ppermute(give, "c", shifted(c_size, 1)))
    total = total.reshape(y_size, z_part * strip, width)
    total = add(
        total[0], *(lax.ppermute(total[k], "y", shifted(y_size, k)) for k in range(1, y_size))
    ).reshape(z_part, strip, width)
    low, top = z % 2, z // (z_size // 2)
    given = lax.dynamic_index_in_dim(total, 1 - low, 0, keepdims=False)
    kept = lax.dynamic_index_in_dim(total, low, 0, keepdims=False)
    total = add(kept, lax.ppermute(given, "z", [(i, i ^ 1) for i in range(z_size)]))
    total = total.reshape(strip, 2, width // 2)
    given = lax.dynamic_index_in_dim(total, 1 - top, 1, keepdims=False)
    kept = lax.dynamic_index_in_dim(total, top, 1, keepdims=False)
    total = add(kept, lax.ppermute(given, "z", [(i, (i + z_size // 2) % z_size) for i in range(z_size)]))
    total = total.reshape(strip, 2, width // 4)
    final = 0.0
    for flip in range(2):
        pairs = []
        for z_from in range(z_size):
            bit = (z_from // 2 % 2) ^ flip
            for x_from in range(x_size):
                to_z, to_x = z_part * x_from + z_from % 2, z_from // (z_size // 2) * 2 + bit
                pairs.append((z_from * x_size + x_from, to_z * x_size + to_x))
        chunk = lax.dynamic_index_in_dim(total, (z // 2 % 2) ^ flip, 1, keepdims=False)
        final = final + lax.ppermute(chunk, ("z", "x"), pairs).astype(F32)
    return final.T


def exchange_images(own_images, table, place, sizes):
    z_size, y_size, c_size = sizes
    blocks = own_images.shape[0]
    up = down = own_images
    steps = [[(0, own_images)]]
    for k in range(1, z_size // 2):
        up = lax.ppermute(up, "z", shifted(z_size, 1))
        down = lax.ppermute(down, "z", shifted(z_size, -1))
        steps.append([(k, up), (-k, down)])
    up = lax.ppermute(up[: blocks // 2], "z", shifted(z_size, 1))
    down = lax.ppermute(down[blocks // 2 :], "z", shifted(z_size, -1))
    steps[-1].append((z_size // 2, jnp.concatenate([up, down], axis=0)))
    groups = []
    for group in steps:
        count = len(group)
        shape = (count,) + own_images.shape[1:]
        picked = pl.pallas_call(
            functools.partial(pick_kernel, steps=[k for k, _ in group], sizes=sizes),
            out_shape=[jax.ShapeDtypeStruct(shape, BF16)] * (y_size * c_size),
            in_specs=[whole(pltpu.SMEM)] * 2 + [whole(pl.ANY)] * count,
            out_specs=[whole(pl.ANY)] * (y_size * c_size),
            scratch_shapes=[pltpu.SemaphoreType.DMA((y_size * c_size * count,))],
            name="pick",
        )(table, place, *(v for _, v in group))
        got = [picked[0]]
        for n in range(1, y_size * c_size):
            dy, dc = n // c_size, n % c_size
            pairs = [
                (y * c_size + c, (y + dy) % y_size * c_size + (c + dc) % c_size)
                for y in range(y_size)
                for c in range(c_size)
            ]
            got.append(lax.ppermute(picked[n], ("y", "c"), pairs))
        groups.append(got)
    return groups


def solution(mesh):
    x_size = mesh.shape["replica"]
    c_size = 2
    z_size = 2 * x_size
    y_size = mesh.shape["dp"] // (z_size * c_size)
    fine = Mesh(mesh.devices.reshape(z_size, y_size, c_size, x_size), ("z", "y", "c", "x"))
    placed = (P(DP, "x", None, None), P(), P(DP, None, None), P(DP, None), P(), P(), P())
    return jax.shard_map(
        on_device,
        mesh=fine,
        in_specs=placed,
        out_specs=(P(DP, "x"), P("x", DP)),
        check_vma=False,
    )
```

```python
import functools

import jax
import jax.numpy as jnp
from jax import lax
from jax.experimental import pallas as pl
from jax.experimental.pallas import tpu as pltpu
from jax.sharding import Mesh, PartitionSpec as P

EPSILON = 1e-06
DP = ("z", "y", "c")
GROUP = 4
EXTRA = 128
F32 = jnp.float32
BF16 = jnp.bfloat16


def dot(a, b, contract):
    return lax.dot_general(a, b, ((contract[:1], contract[1:]), ((), ())), preferred_element_type=F32)


def unit_rows(values):
    inverse = lax.rsqrt(jnp.sum(values * values, axis=-1, keepdims=True) + EPSILON)
    return (values * inverse, inverse)


def shifted(size, shift):
    return [(i, (i + shift) % size) for i in range(size)]


def loss_and_weight(logits):
    small = jnp.exp(-jnp.abs(logits))
    share = 1.0 / (1.0 + small)
    weight = jnp.where(logits >= 0, share, small * share)
    return (jnp.maximum(logits, 0.0) + jnp.log1p(small), weight)


def project_kernel(features, weight, out, acc):
    step = pl.program_id(0)

    @pl.when(step == 0)
    def _():
        acc[...] = jnp.zeros_like(acc)

    acc[...] += dot(features[...], weight[...], (1, 0))

    @pl.when(step == pl.num_programs(0) - 1)
    def _():
        unit, inverse = unit_rows(acc[...])
        width = unit.shape[1]
        out[:, :width] = unit.astype(BF16)
        first = inverse.astype(BF16).astype(F32)
        second = (inverse - first).astype(BF16).astype(F32)
        third = inverse - first - second
        lane = lax.broadcasted_iota(jnp.int32, (unit.shape[0], EXTRA), 1)
        terms = jnp.where(lane == 0, first, jnp.where(lane == 1, second, jnp.where(lane == 2, third, 0.0)))
        out[:, width:] = terms.astype(BF16)


def pair_kernel(sources, slots, counts, place, scale_bias, *refs, starts, own):
    quarters = 4
    texts, refs = refs[:quarters], refs[quarters:]
    if own:
        own_images, image_docs, text_docs, *refs = refs
    arriving, refs = refs[: len(starts)], refs[len(starts) :]
    chunks, pair_loss, refs = refs[0], refs[1], refs[2:]
    if own:
        own_loss, *refs = refs
    text_all, arrived, acc, sems = refs
    blocks, block_rows, width = text_all.shape
    width -= EXTRA
    piece_rows = block_rows // quarters
    part = width // quarters
    scale, bias = scale_bias[0], scale_bias[1]
    copies = []
    for n, (ref, at) in enumerate(zip(arriving, starts)):
        count = ref.shape[0] // 2
        half = ref.at[pl.ds(0 if own else count, count)]
        copies.append(pltpu.make_async_copy(half, arrived.at[pl.ds(at, count)], sems.at[n]))
        copies[-1].start()
    for k in range(quarters):
        to = pl.multiple_of(lax.rem(place[0] - k + quarters, quarters) * piece_rows, piece_rows)
        text_all[:, pl.ds(to, piece_rows), :] = texts[k][...].reshape(blocks, piece_rows, width + EXTRA)
    pair_loss[...] = jnp.zeros_like(pair_loss)
    for copy in copies:
        copy.wait()

    def each_block(t, carry):
        text = text_all[t, :, :width]
        if own:
            images = own_images[t]
            logits = scale * dot(text, images, (1, 1)) + bias
            same = text_docs[t] == image_docs[t]
            sign = jnp.where(same, 1.0, -1.0)
            loss, weight = loss_and_weight(-sign * logits)
            own_loss[pl.ds(t, 1)] = jnp.sum(loss, axis=0, keepdims=True)[None]
            acc[...] = dot((-sign * weight).astype(BF16), images, (1, 0))
        else:
            acc[...] = jnp.zeros_like(acc)
        count = counts[t]

        def each_group(g, inner):
            held = [slots[t, g * GROUP + i] for i in range(GROUP)]
            rows = jnp.concatenate([arrived[held[i]] for i in range(GROUP)], axis=0)
            values = scale * dot(text, rows, (1, 1)) + bias
            terms, shares = loss_and_weight(values)
            sums = jnp.sum(terms, axis=0, keepdims=True)
            left = (count - g * GROUP) * piece_rows
            live = lax.broadcasted_iota(jnp.int32, shares.shape, 1) < left
            shares = jnp.where(live, shares, 0.0).astype(BF16)
            acc[...] += dot(shares, rows, (1, 0))
            for i in range(GROUP):

                @pl.when(g * GROUP + i < count)
                def _():
                    source = sources[t, g * GROUP + i]
                    pair_loss[pl.ds(source, 1)] = sums[:, i * piece_rows : (i + 1) * piece_rows][None]

            return inner

        lax.fori_loop(0, (count + GROUP - 1) // GROUP, each_group, 0)
        inverse = jnp.sum(text_all[t, :, width:].astype(F32), axis=-1, keepdims=True)
        unit = text.astype(F32)
        grad = scale * acc[...]
        along = jnp.sum(unit * grad, axis=-1, keepdims=True)
        acc[...] = (grad - unit * along) * inverse
        for k in range(quarters):
            start = pl.multiple_of(lax.rem(place[0] + k, quarters) * part, part)
            values = acc[:, pl.ds(start, part)].astype(BF16)
            for j in range(quarters):
                chunks[k, j, pl.ds(t, 1)] = values[j * piece_rows : (j + 1) * piece_rows][None]
        return carry

    lax.fori_loop(0, blocks, each_block, 0)


def pick_kernel(table, place, *refs, step, sizes):
    z_size, y_size, c_size = sizes
    to_refs, sems = refs[-1 - y_size : -1], refs[-1]
    from_ref = refs[0]
    count = from_ref.shape[0]
    back = jnp.where(place[2] == 0, step, z_size - step)
    z = lax.rem(place[3] - back + z_size, z_size)
    copies = []
    for dy in range(y_size):
        y = lax.rem(place[1] + dy, y_size)
        for to in range(c_size):
            for j in range(count):
                source = z * c_size + lax.rem(place[2] + j, c_size)
                block = table[source, y * c_size + lax.rem(place[2] + to, c_size)]
                n = to * count + j
                sem = sems.at[dy * c_size * count + n]
                copies.append(pltpu.make_async_copy(from_ref.at[j, block], to_refs[dy].at[n], sem))
    for copy in copies:
        copy.start()
    for copy in copies:
        copy.wait()


def head_kernel(place, grad_0, grad_1, grad_2, grad_3, feats, keep, give, turned, *, sizes, strip):
    z_part, y_size, c_size = sizes

    @pl.when(pl.program_id(0) == 0)
    def _():
        total = sum(g[...].astype(F32) for g in (grad_0, grad_1, grad_2, grad_3))
        flipped = total.T.astype(BF16)
        for zz in range(z_part):
            for y in range(y_size):
                for c in range(c_size):
                    block = flipped[((zz * y_size + y) * c_size + c) * strip :][:strip]
                    y_rel = lax.rem(y - place[1] + y_size, y_size)
                    c_rel = lax.rem(c - place[2] + c_size, c_size)
                    to = ((c_rel * y_size + y_rel) * z_part + zz) * strip
                    turned[pl.ds(pl.multiple_of(to, strip), strip)] = block

    half = keep.shape[0]
    total = dot(turned[...], feats[...], (1, 0)).astype(BF16)
    keep[...] = total[:half]
    give[...] = total[half:]


def whole(memory=pltpu.VMEM):
    return pl.BlockSpec(memory_space=memory)


def on_device(
    text_features, head_weight, image_embeds, doc_ids, hard_lists, logit_scale, logit_bias
):
    z_size, y_size, c_size, x_size = (lax.axis_size(name) for name in ("z", "y", "c", "x"))
    z, y, c, x = (lax.axis_index(name) for name in ("z", "y", "c", "x"))
    dp_count = z_size * y_size * c_size
    dp_index = (z * y_size + y) * c_size + c
    blocks, _, piece_rows, feat_width = text_features.shape
    block_rows = image_embeds.shape[1]
    emb_width = head_weight.shape[1]
    rows = blocks * piece_rows
    part = emb_width // x_size
    strip = emb_width // dp_count
    block_iota = jnp.arange(blocks, dtype=jnp.int32)
    peer_iota = jnp.arange(dp_count, dtype=jnp.int32)
    place = jnp.stack([x, y, c, z]).astype(jnp.int32)
    features = text_features.reshape(rows, feat_width)
    feats = lax.all_gather(features, "x", axis=0, tiled=False)

    owners = jnp.where(hard_lists >= 0, hard_lists // blocks, -1).reshape(dp_count, blocks, -1)
    line = owners.reshape(z_size, y_size, c_size, blocks, -1)
    line = lax.dynamic_index_in_dim(line, y, 1, keepdims=False).reshape(z_size * c_size, blocks, -1)
    plane = z * y_size * c_size + jnp.arange(y_size * c_size, dtype=jnp.int32)
    wanted = jnp.any(line[:, None] == plane[:, None, None], axis=3)
    table = jnp.sum(wanted.astype(jnp.int32) * block_iota, axis=2)

    own_images = lax.dynamic_slice_in_dim(image_embeds, x * piece_rows, piece_rows, 1)
    own_images = unit_rows(own_images.astype(F32))[0].astype(BF16)
    groups = exchange_images(own_images, table, place, (z_size, y_size, c_size))

    tile = min(1024, feat_width)
    text_emb = pl.pallas_call(
        project_kernel,
        grid=(feat_width // tile,),
        out_shape=jax.ShapeDtypeStruct((rows, emb_width + EXTRA), BF16),
        in_specs=[
            pl.BlockSpec((rows, tile), lambda i: (0, i)),
            pl.BlockSpec((tile, emb_width), lambda i: (i, 0)),
        ],
        out_specs=pl.BlockSpec((rows, emb_width + EXTRA), lambda i: (0, 0)),
        scratch_shapes=[pltpu.VMEM((rows, emb_width), F32)],
        compiler_params=pltpu.CompilerParams(vmem_limit_bytes=32 << 20),
        cost_estimate=pl.CostEstimate(
            flops=2 * rows * feat_width * emb_width, bytes_accessed=12 << 20, transcendentals=0
        ),
        name="project",
    )(features, head_weight)
    texts = [text_emb]
    for _ in range(1, x_size):
        texts.append(lax.ppermute(texts[-1], "x", shifted(x_size, 1)))

    arriving, starts, turns = [], [], 0
    for group in groups:
        arriving += group
        starts += [n * z_size + turns for n in range(len(group))]
        turns += group[0].shape[0] // c_size
    away = jnp.where(c == 0, z - peer_iota // (y_size * c_size), peer_iota // (y_size * c_size) - z) % z_size
    over_y = (y - peer_iota // c_size) % y_size
    over_c = (c - peer_iota) % c_size
    ends = (away == 0) | (away == z_size // 2)
    have = jnp.where(ends, over_c == 0, away < z_size // 2)
    turn = jnp.where(ends, away * 2 - (away > 0), 2 * away - 1 + over_c)
    slot_of = over_y * z_size + turn

    text_docs = doc_ids.reshape(blocks, block_rows, 1)
    image_docs = lax.dynamic_slice_in_dim(doc_ids, x * piece_rows, piece_rows, 1)[:, None]
    scale_bias = jnp.stack([logit_scale, logit_bias])

    def pairs(holder, pieces, own):
        hit = owners == holder
        which = jnp.sum(hit * (hard_lists % blocks).reshape(owners.shape), axis=(1, 2))
        mine = (jnp.any(hit, axis=(1, 2)) & have)[None] & (which[None] == block_iota[:, None])
        before = peer_iota[None] < peer_iota[:, None]
        order = jnp.sum((mine[:, None] & before).astype(jnp.int32), axis=2)
        counts = jnp.sum(mine.astype(jnp.int32), axis=1)
        at = mine[:, None] & (order[:, None] == peer_iota[:, None])
        sources = jnp.sum(jnp.where(at, peer_iota, 0), axis=2)
        slots = jnp.sum(jnp.where(at, slot_of, 0), axis=2)
        extra = [own_images, image_docs, text_docs] if own else []
        losses = [jax.ShapeDtypeStruct((blocks, 1, piece_rows), F32)] if own else []
        return pl.pallas_call(
            functools.partial(pair_kernel, starts=starts, own=own),
            out_shape=[
                jax.ShapeDtypeStruct((x_size, x_size, blocks, piece_rows, part), BF16),
                jax.ShapeDtypeStruct((dp_count, 1, piece_rows), F32),
            ]
            + losses,
            in_specs=[whole(pltpu.SMEM)] * 5
            + [whole()] * (x_size + len(extra))
            + [whole(pl.ANY)] * len(arriving),
            out_specs=[whole()] * (2 + len(losses)),
            scratch_shapes=[
                pltpu.VMEM((blocks, block_rows, emb_width + EXTRA), BF16),
                pltpu.VMEM((y_size * z_size, piece_rows, emb_width), BF16),
                pltpu.VMEM((block_rows, emb_width), F32),
                pltpu.SemaphoreType.DMA((len(arriving),)),
            ],
            compiler_params=pltpu.CompilerParams(vmem_limit_bytes=56 << 20),
            cost_estimate=pl.CostEstimate(flops=4 << 30, bytes_accessed=10 << 20, transcendentals=2 << 20),
            name="pairs",
        )(sources, slots, counts, place, scale_bias, *pieces, *extra, *arriving)

    other_texts = [lax.ppermute(piece, "c", shifted(c_size, 1)) for piece in texts]
    other_chunks, other_loss = pairs(dp_index + 1 - 2 * c, other_texts, False)
    chunks, pair_loss, own_loss = pairs(dp_index, texts, True)

    taken = lax.ppermute(other_chunks, "c", shifted(c_size, 1))
    grads = []
    for k in range(x_size):
        total = (chunks[k].astype(F32) + taken[k].astype(F32)).astype(BF16).reshape(x_size * rows, part)
        grads.append(lax.ppermute(total, "x", shifted(x_size, k)) if k else total)
    z_part = z_size // x_size
    half = part // c_size
    keep, give = pl.pallas_call(
        functools.partial(head_kernel, sizes=(z_part, y_size, c_size), strip=strip),
        grid=(feat_width // tile,),
        out_shape=(
            jax.ShapeDtypeStruct((half, feat_width), BF16),
            jax.ShapeDtypeStruct((half, feat_width), BF16),
        ),
        in_specs=[whole(pltpu.SMEM)]
        + [whole()] * 4
        + [pl.BlockSpec((x_size * rows, tile), lambda i: (0, i))],
        out_specs=(
            pl.BlockSpec((half, tile), lambda i: (0, i)),
            pl.BlockSpec((half, tile), lambda i: (0, i)),
        ),
        scratch_shapes=[pltpu.VMEM((part, x_size * rows), BF16)],
        compiler_params=pltpu.CompilerParams(vmem_limit_bytes=48 << 20),
        cost_estimate=pl.CostEstimate(
            flops=2 * rows * feat_width * emb_width, bytes_accessed=16 << 20, transcendentals=0
        ),
        name="head",
    )(place, *grads, feats.reshape(x_size * rows, feat_width))

    returned = lax.all_to_all(
        jnp.concatenate([pair_loss, other_loss], axis=1), DP, split_axis=0, concat_axis=0, tiled=True
    )
    swapped = returned.reshape(-1, c_size, 2, piece_rows)[:, ::-1, 1].reshape(dp_count, piece_rows)
    returned = returned[:, 0] + swapped
    my_owners = lax.dynamic_index_in_dim(owners, dp_index, 0, keepdims=False)
    asked = jnp.any(my_owners[None] == peer_iota[:, None, None], axis=2)
    remote_loss = jnp.sum(jnp.where(asked[..., None], returned[:, None], 0.0), axis=0)
    row_loss = (own_loss.reshape(blocks, piece_rows) + remote_loss) / block_rows
    return (row_loss, add_over_dp(keep, give, (z_size, y_size, c_size, x_size), z, strip))


def add_over_dp(keep, give, sizes, z, strip):
    z_size, y_size, c_size, x_size = sizes
    z_part = z_size // x_size
    width = keep.shape[1]

    def add(*values):
        return sum(v.astype(F32) for v in values).astype(BF16)

    total = add(keep, lax.ppermute(give, "c", shifted(c_size, 1)))
    total = total.reshape(y_size, z_part * strip, width)
    total = add(
        total[0], *(lax.ppermute(total[k], "y", shifted(y_size, k)) for k in range(1, y_size))
    ).reshape(z_part, strip, width)
    low, top = z % 2, z // (z_size // 2)
    given = lax.dynamic_index_in_dim(total, 1 - low, 0, keepdims=False)
    kept = lax.dynamic_index_in_dim(total, low, 0, keepdims=False)
    total = add(kept, lax.ppermute(given, "z", [(i, i ^ 1) for i in range(z_size)]))
    total = total.reshape(strip, 2, width // 2)
    given = lax.dynamic_index_in_dim(total, 1 - top, 1, keepdims=False)
    kept = lax.dynamic_index_in_dim(total, top, 1, keepdims=False)
    total = add(kept, lax.ppermute(given, "z", [(i, (i + z_size // 2) % z_size) for i in range(z_size)]))
    total = total.reshape(strip, 2, width // 4)
    final = 0.0
    for flip in range(2):
        pairs = []
        for z_from in range(z_size):
            bit = (z_from // 2 % 2) ^ flip
            for x_from in range(x_size):
                to_z, to_x = z_part * x_from + z_from % 2, z_from // (z_size // 2) * 2 + bit
                pairs.append((z_from * x_size + x_from, to_z * x_size + to_x))
        chunk = lax.dynamic_index_in_dim(total, (z // 2 % 2) ^ flip, 1, keepdims=False)
        final = final + lax.ppermute(chunk, ("z", "x"), pairs).astype(F32)
    return final.T


def exchange_images(own_images, table, place, sizes):
    z_size, y_size, c_size = sizes
    onward = []
    for z in range(z_size):
        onward.append((z * c_size, (z + 1) % z_size * c_size))
        onward.append((z * c_size + 1, (z - 1) % z_size * c_size + 1))
    moving = jnp.stack([own_images, lax.ppermute(own_images, "c", shifted(c_size, 1))])
    groups = []
    for step in range(z_size // 2 + 1):
        if step == 0:
            here = own_images[None]
        else:
            moving = moving[:1] if step == z_size // 2 else moving
            here = moving = lax.ppermute(moving, ("z", "c"), onward)
        shape = (c_size * here.shape[0],) + own_images.shape[1:]
        picked = pl.pallas_call(
            functools.partial(pick_kernel, step=step, sizes=sizes),
            out_shape=[jax.ShapeDtypeStruct(shape, BF16)] * y_size,
            in_specs=[whole(pltpu.SMEM)] * 2 + [whole()],
            out_specs=[whole(pl.ANY)] * y_size,
            scratch_shapes=[pltpu.SemaphoreType.DMA((y_size * shape[0],))],
            name="pick",
        )(table, place, here)
        groups.append(
            [picked[0]] + [lax.ppermute(picked[n], "y", shifted(y_size, n)) for n in range(1, y_size)]
        )
    return groups


def solution(mesh):
    x_size = mesh.shape["replica"]
    c_size = 2
    z_size = 2 * x_size
    y_size = mesh.shape["dp"] // (z_size * c_size)
    fine = Mesh(mesh.devices.reshape(z_size, y_size, c_size, x_size), ("z", "y", "c", "x"))
    placed = (P(DP, "x", None, None), P(), P(DP, None, None), P(DP, None), P(), P(), P())
    return jax.shard_map(
        on_device,
        mesh=fine,
        in_specs=placed,
        out_specs=(P(DP, "x"), P("x", DP)),
        check_vma=False,
    )
```

```python
import functools

import jax
import jax.numpy as jnp
from jax import lax
from jax.experimental import pallas as pl
from jax.experimental.pallas import tpu as pltpu
from jax.sharding import Mesh, PartitionSpec as P

EPSILON = 1e-06
DP = ("z", "y", "c")
GROUP = 2
EXTRA = 128
F32 = jnp.float32
BF16 = jnp.bfloat16


def dot(a, b, contract):
    return lax.dot_general(a, b, ((contract[:1], contract[1:]), ((), ())), preferred_element_type=F32)


def unit_rows(values):
    inverse = lax.rsqrt(jnp.sum(values * values, axis=-1, keepdims=True) + EPSILON)
    return (values * inverse, inverse)


def shifted(size, shift):
    return [(i, (i + shift) % size) for i in range(size)]


def loss_and_weight(logits):
    small = jnp.exp(-jnp.abs(logits))
    share = 1.0 / (1.0 + small)
    weight = jnp.where(logits >= 0, share, small * share)
    return (jnp.maximum(logits, 0.0) + jnp.log1p(small), weight)


def project_kernel(features, weight, *refs):
    out, acc = refs[-2:]
    step = pl.program_id(0)

    @pl.when(step == 0)
    def _():
        acc[...] = jnp.zeros_like(acc)

    acc[...] += dot(features[...], weight[...], (1, 0))

    @pl.when(step == pl.num_programs(0) - 1)
    def _():
        unit, inverse = unit_rows(acc[...])
        width = unit.shape[1]
        text = unit.astype(BF16)
        first = inverse.astype(BF16).astype(F32)
        second = (inverse - first).astype(BF16).astype(F32)
        third = inverse - first - second
        lane = lax.broadcasted_iota(jnp.int32, (unit.shape[0], EXTRA), 1)
        terms = jnp.where(lane == 0, first, jnp.where(lane == 1, second, jnp.where(lane == 2, third, 0.0)))
        terms = terms.astype(BF16)
        for k in range(out.shape[0]):
            out[k, :, :width] = text
            out[k, :, width:] = terms


def add_tiles(t, text, acc, sources, slots, counts, scale_bias, arrived, pair_loss):
    scale, bias = scale_bias[0], scale_bias[1]
    piece_rows = arrived.shape[1]
    count = counts[t]

    def each_group(g, carry):
        held = [slots[t, g * GROUP + i] for i in range(GROUP)]
        rows = jnp.concatenate([arrived[held[i]] for i in range(GROUP)], axis=0)
        values = scale * dot(text, rows, (1, 1)) + bias
        terms, shares = loss_and_weight(values)
        sums = jnp.sum(terms, axis=0, keepdims=True)
        left = (count - g * GROUP) * piece_rows
        live = lax.broadcasted_iota(jnp.int32, shares.shape, 1) < left
        shares = jnp.where(live, shares, 0.0).astype(BF16)
        acc[...] += dot(shares, rows, (1, 0))
        for i in range(GROUP):

            @pl.when(g * GROUP + i < count)
            def _():
                source = sources[t, g * GROUP + i]
                pair_loss[pl.ds(source, 1)] = sums[:, i * piece_rows : (i + 1) * piece_rows][None]

        return carry

    lax.fori_loop(0, (count + GROUP - 1) // GROUP, each_group, 0)


def bring(arriving, arrived, starts, sems, half):
    copies = []
    for n, (ref, at) in enumerate(zip(arriving, starts)):
        count = ref.shape[0] // 2
        rows = ref.at[pl.ds(half * count, count)]
        copies.append(pltpu.make_async_copy(rows, arrived.at[pl.ds(at, count)], sems.at[n]))
    return copies


def pair_kernel(sources, slots, counts, place, scale_bias, texts, *refs, starts, own):
    if own:
        own_images, image_docs, text_docs, *refs = refs
    arriving, refs = refs[: len(starts)], refs[len(starts) :]
    chunks, pair_loss, *refs = refs
    if own:
        own_loss, *refs = refs
    acc, arrived, sems = refs
    t = pl.program_id(0)
    quarters, _, _, piece_rows, part = chunks.shape
    width = quarters * part
    copies = bring(arriving, arrived, starts, sems, 0 if own else 1)

    @pl.when(t == 0)
    def _():
        for copy in copies:
            copy.start()
        pair_loss[...] = jnp.zeros_like(pair_loss)

    scale, bias = scale_bias[0], scale_bias[1]
    block = texts[...].reshape(quarters * piece_rows, width + EXTRA)
    text = block[:, :width]
    if own:
        images = own_images[0]
        logits = scale * dot(text, images, (1, 1)) + bias
        same = text_docs[0] == image_docs[0]
        sign = jnp.where(same, 1.0, -1.0)
        loss, weight = loss_and_weight(-sign * logits)
        own_loss[0] = jnp.sum(loss, axis=0, keepdims=True)
        acc[...] = dot((-sign * weight).astype(BF16), images, (1, 0))
    else:
        acc[...] = jnp.zeros_like(acc)

    @pl.when(t == 0)
    def _():
        for copy in copies:
            copy.wait()

    add_tiles(t, text, acc, sources, slots, counts, scale_bias, arrived, pair_loss)
    inverse = jnp.sum(block[:, width:].astype(F32), axis=-1, keepdims=True)
    unit = text.astype(F32)
    grad = scale * acc[...]
    along = jnp.sum(unit * grad, axis=-1, keepdims=True)
    acc[...] = (grad - unit * along) * inverse
    for k in range(quarters):
        start = pl.multiple_of(lax.rem(place[0] + k, quarters) * part, part)
        values = acc[:, pl.ds(start, part)].astype(BF16)
        for j in range(quarters):
            chunks[k, j, 0] = values[j * piece_rows : (j + 1) * piece_rows]


def pick_kernel(table, place, from_ref, *refs, step, sizes, onward):
    z_size, y_size, c_size = sizes
    sems = refs[-1]
    outs = y_size + (onward > 0)
    to_refs = refs[-1 - outs : -1]
    count = from_ref.shape[0]
    back = jnp.where(place[2] == 0, step, z_size - step)
    z = lax.rem(place[3] - back + z_size, z_size)
    copies = []
    if onward:
        copies.append(pltpu.make_async_copy(from_ref.at[pl.ds(0, onward)], to_refs[-1], sems.at[0]))
    for dy in range(y_size):
        y = lax.rem(place[1] + dy, y_size)
        for to in range(c_size):
            for j in range(count):
                source = z * c_size + lax.rem(place[2] + j, c_size)
                block = table[source, y * c_size + lax.rem(place[2] + to, c_size)]
                n = to * count + j
                sem = sems.at[1 + dy * c_size * count + n]
                copies.append(pltpu.make_async_copy(from_ref.at[j, block], to_refs[dy].at[n], sem))
    for copy in copies:
        copy.start()
    for copy in copies:
        copy.wait()


def head_kernel(place, grad_0, grad_1, grad_2, grad_3, feats, first_done, keep, give, turned, *, sizes, strip):
    z_part, y_size, c_size = sizes

    @pl.when(pl.program_id(0) == 0)
    def _():
        total = sum(g[...].astype(F32) for g in (grad_0, grad_1, grad_2, grad_3))
        flipped = total.T.astype(BF16)
        for zz in range(z_part):
            for y in range(y_size):
                for c in range(c_size):
                    block = flipped[((zz * y_size + y) * c_size + c) * strip :][:strip]
                    y_rel = lax.rem(y - place[1] + y_size, y_size)
                    c_rel = lax.rem(c - place[2] + c_size, c_size)
                    to = ((c_rel * y_size + y_rel) * z_part + zz) * strip
                    turned[pl.ds(pl.multiple_of(to, strip), strip)] = block

    half = keep.shape[0]
    total = dot(turned[...], feats[...], (1, 0)).astype(BF16)
    keep[...] = total[:half]
    give[...] = total[half:]


def whole(memory=pltpu.VMEM):
    return pl.BlockSpec(memory_space=memory)


def on_device(
    text_features, head_weight, image_embeds, doc_ids, hard_lists, logit_scale, logit_bias
):
    z_size, y_size, c_size, x_size = (lax.axis_size(name) for name in ("z", "y", "c", "x"))
    z, y, c, x = (lax.axis_index(name) for name in ("z", "y", "c", "x"))
    dp_count = z_size * y_size * c_size
    dp_index = (z * y_size + y) * c_size + c
    blocks, _, piece_rows, feat_width = text_features.shape
    block_rows = image_embeds.shape[1]
    emb_width = head_weight.shape[1]
    rows = blocks * piece_rows
    part = emb_width // x_size
    strip = emb_width // dp_count
    block_iota = jnp.arange(blocks, dtype=jnp.int32)
    peer_iota = jnp.arange(dp_count, dtype=jnp.int32)
    place = jnp.stack([x, y, c, z]).astype(jnp.int32)
    features = text_features.reshape(rows, feat_width)
    feats = lax.all_gather(features, "x", axis=0, tiled=False)

    owners = jnp.where(hard_lists >= 0, hard_lists // blocks, -1).reshape(dp_count, blocks, -1)
    line = owners.reshape(z_size, y_size, c_size, blocks, -1)
    line = lax.dynamic_index_in_dim(line, y, 1, keepdims=False).reshape(z_size * c_size, blocks, -1)
    plane = z * y_size * c_size + jnp.arange(y_size * c_size, dtype=jnp.int32)
    wanted = jnp.any(line[:, None] == plane[:, None, None], axis=3)
    table = jnp.sum(wanted.astype(jnp.int32) * block_iota, axis=2)

    own_images = lax.dynamic_slice_in_dim(image_embeds, x * piece_rows, piece_rows, 1)
    own_images = unit_rows(own_images.astype(F32))[0].astype(BF16)
    groups = exchange_images(own_images, table, place, (z_size, y_size, c_size))

    tile = min(1024, feat_width)
    text_emb = pl.pallas_call(
        project_kernel,
        grid=(feat_width // tile,),
        out_shape=jax.ShapeDtypeStruct((x_size * c_size, rows, emb_width + EXTRA), BF16),
        in_specs=[
            pl.BlockSpec((rows, tile), lambda i: (0, i)),
            pl.BlockSpec((tile, emb_width), lambda i: (i, 0)),
        ]
        + [whole(pl.ANY)],
        out_specs=pl.BlockSpec((x_size * c_size, rows, emb_width + EXTRA), lambda i: (0, 0, 0)),
        scratch_shapes=[pltpu.VMEM((rows, emb_width), F32)],
        compiler_params=pltpu.CompilerParams(vmem_limit_bytes=60 << 20),
        cost_estimate=pl.CostEstimate(flops=1, bytes_accessed=1, transcendentals=0),
        name="project",
    )(features, head_weight, groups[0][0])
    texts = lax.all_to_all(text_emb, ("x", "c"), split_axis=0, concat_axis=0, tiled=True)
    texts = texts.reshape(x_size, c_size, rows, emb_width + EXTRA)

    arrays, starts, slot_base, turns = [], [], [], 0
    for group in groups:
        count = group[0].shape[0] // c_size
        slot_base.append(turns)
        for array in group:
            arrays.append(array)
            starts.append(turns)
            turns += count
    away = jnp.where(c == 0, z - peer_iota // (y_size * c_size), peer_iota // (y_size * c_size) - z) % z_size
    over_y = (y - peer_iota // c_size) % y_size
    over_c = (c - peer_iota) % c_size
    ends = (away == 0) | (away == z_size // 2)
    have = jnp.where(ends, over_c == 0, away < z_size // 2)
    base = sum(jnp.where(away == k, b, 0) for k, b in enumerate(slot_base))
    slot_of = base + jnp.where(ends, over_y, over_y * c_size + over_c)

    text_docs = doc_ids.reshape(blocks, block_rows, 1)
    image_docs = lax.dynamic_slice_in_dim(doc_ids, x * piece_rows, piece_rows, 1)[:, None]
    scale_bias = jnp.stack([logit_scale, logit_bias])

    def lists(holder, here):
        hit = owners == holder
        which = jnp.sum(hit * (hard_lists % blocks).reshape(owners.shape), axis=(1, 2))
        mine = (jnp.any(hit, axis=(1, 2)) & here)[None] & (which[None] == block_iota[:, None])
        before = peer_iota[None] < peer_iota[:, None]
        order = jnp.sum((mine[:, None] & before).astype(jnp.int32), axis=2)
        at = mine[:, None] & (order[:, None] == peer_iota[:, None])
        sources = jnp.sum(jnp.where(at, peer_iota, 0), axis=2)
        return sources, jnp.sum(jnp.where(at, slot_of, 0), axis=2), jnp.sum(mine.astype(jnp.int32), axis=1)

    loss_shape = jax.ShapeDtypeStruct((dp_count, 1, piece_rows), F32)

    def pairs(holder, pieces, own):
        extra, extra_specs, losses, loss_specs = [], [], [], []
        if own:
            extra = [own_images, image_docs, text_docs]
            extra_specs = [pl.BlockSpec((1,) + v.shape[1:], lambda t: (t, 0, 0)) for v in extra]
            losses = [jax.ShapeDtypeStruct((blocks, 1, piece_rows), F32)]
            loss_specs = [pl.BlockSpec((1, 1, piece_rows), lambda t: (t, 0, 0))]
        return pl.pallas_call(
            functools.partial(pair_kernel, starts=starts, own=own),
            grid=(blocks,),
            out_shape=[
                jax.ShapeDtypeStruct((x_size, x_size, blocks, piece_rows, part), BF16),
                loss_shape,
            ]
            + losses,
            in_specs=[whole(pltpu.SMEM)] * 5
            + [pl.BlockSpec((x_size, 1, piece_rows, emb_width + EXTRA), lambda t: (0, t, 0, 0))]
            + extra_specs
            + [whole(pl.ANY)] * len(arrays),
            out_specs=[
                pl.BlockSpec((x_size, x_size, 1, piece_rows, part), lambda t: (0, 0, t, 0, 0)),
                pl.BlockSpec(loss_shape.shape, lambda t: (0, 0, 0)),
            ]
            + loss_specs,
            scratch_shapes=[
                pltpu.VMEM((block_rows, emb_width), F32),
                pltpu.VMEM((turns, piece_rows, emb_width), BF16),
                pltpu.SemaphoreType.DMA((len(arrays),)),
            ],
            compiler_params=pltpu.CompilerParams(vmem_limit_bytes=32 << 20),
            cost_estimate=pl.CostEstimate(flops=1, bytes_accessed=1, transcendentals=0),
            name="pairs",
        )(
            *lists(holder, have),
            place,
            scale_bias,
            pieces.reshape(x_size, blocks, piece_rows, emb_width + EXTRA),
            *extra,
            *arrays,
        )

    other_texts = lax.dynamic_index_in_dim(texts, 1 - c, 1, keepdims=False)
    other_chunks, other_loss = pairs(dp_index + 1 - 2 * c, other_texts, False)
    own_texts = lax.dynamic_index_in_dim(texts, c, 1, keepdims=False)
    chunks, pair_loss, own_loss = pairs(dp_index, own_texts, True)

    returned = lax.all_to_all(
        jnp.concatenate([pair_loss, other_loss], axis=1), DP, split_axis=0, concat_axis=0, tiled=True
    )

    taken = lax.ppermute(other_chunks, "c", shifted(c_size, 1))
    grads = []
    for k in range(x_size):
        total = (chunks[k].astype(F32) + taken[k].astype(F32)).astype(BF16).reshape(x_size * rows, part)
        grads.append(lax.ppermute(total, "x", shifted(x_size, k)) if k else total)
    z_part = z_size // x_size
    half = part // c_size
    keep, give = pl.pallas_call(
        functools.partial(head_kernel, sizes=(z_part, y_size, c_size), strip=strip),
        grid=(feat_width // tile,),
        out_shape=(
            jax.ShapeDtypeStruct((half, feat_width), BF16),
            jax.ShapeDtypeStruct((half, feat_width), BF16),
        ),
        in_specs=[whole(pltpu.SMEM)]
        + [whole()] * 4
        + [pl.BlockSpec((x_size * rows, tile), lambda i: (0, i)), whole(pl.ANY)],
        out_specs=(
            pl.BlockSpec((half, tile), lambda i: (0, i)),
            pl.BlockSpec((half, tile), lambda i: (0, i)),
        ),
        scratch_shapes=[pltpu.VMEM((part, x_size * rows), BF16)],
        compiler_params=pltpu.CompilerParams(vmem_limit_bytes=60 << 20),
        cost_estimate=pl.CostEstimate(
            flops=2 * rows * feat_width * emb_width, bytes_accessed=16 << 20, transcendentals=0
        ),
        name="head",
    )(place, *grads, feats.reshape(x_size * rows, feat_width), returned)

    swapped = returned.reshape(-1, c_size, 2, piece_rows)[:, ::-1, 1].reshape(dp_count, piece_rows)
    returned = returned[:, 0] + swapped
    my_owners = lax.dynamic_index_in_dim(owners, dp_index, 0, keepdims=False)
    asked = jnp.any(my_owners[None] == peer_iota[:, None, None], axis=2)
    remote_loss = jnp.sum(jnp.where(asked[..., None], returned[:, None], 0.0), axis=0)
    row_loss = (own_loss.reshape(blocks, piece_rows) + remote_loss) / block_rows
    return (row_loss, add_over_dp(keep, give, (z_size, y_size, c_size, x_size), z, strip))


def add_over_dp(keep, give, sizes, z, strip):
    z_size, y_size, c_size, x_size = sizes
    z_part = z_size // x_size
    width = keep.shape[1]

    def add(*values):
        return sum(v.astype(F32) for v in values).astype(BF16)

    total = add(keep, lax.ppermute(give, "c", shifted(c_size, 1)))
    total = total.reshape(y_size, z_part * strip, width)
    total = add(
        total[0], *(lax.ppermute(total[k], "y", shifted(y_size, k)) for k in range(1, y_size))
    ).reshape(z_part, strip, width)
    low, top = z % 2, z // (z_size // 2)
    given = lax.dynamic_index_in_dim(total, 1 - low, 0, keepdims=False)
    kept = lax.dynamic_index_in_dim(total, low, 0, keepdims=False)
    total = add(kept, lax.ppermute(given, "z", [(i, i ^ 1) for i in range(z_size)]))
    total = total.reshape(strip, 2, width // 2)
    given = lax.dynamic_index_in_dim(total, 1 - top, 1, keepdims=False)
    kept = lax.dynamic_index_in_dim(total, top, 1, keepdims=False)
    total = add(kept, lax.ppermute(given, "z", [(i, (i + z_size // 2) % z_size) for i in range(z_size)]))
    total = total.reshape(strip, 2, width // 4)
    final = 0.0
    for flip in range(2):
        pairs = []
        for z_from in range(z_size):
            bit = (z_from // 2 % 2) ^ flip
            for x_from in range(x_size):
                to_z, to_x = z_part * x_from + z_from % 2, z_from // (z_size // 2) * 2 + bit
                pairs.append((z_from * x_size + x_from, to_z * x_size + to_x))
        chunk = lax.dynamic_index_in_dim(total, (z // 2 % 2) ^ flip, 1, keepdims=False)
        final = final + lax.ppermute(chunk, ("z", "x"), pairs).astype(F32)
    return final.T


def exchange_images(own_images, table, place, sizes):
    z_size, y_size, c_size = sizes
    onward = []
    for z in range(z_size):
        onward.append((z * c_size, (z + 1) % z_size * c_size))
        onward.append((z * c_size + 1, (z - 1) % z_size * c_size + 1))
    moving = jnp.stack([own_images, lax.ppermute(own_images, "c", shifted(c_size, 1))])
    groups = []
    last = z_size // 2
    for step in range(last + 1):
        here = own_images[None] if step == 0 else lax.ppermute(moving, ("z", "c"), onward)
        keeps = 0 if step in (0, last) else 1 if step == last - 1 else c_size
        shape = (c_size * here.shape[0],) + own_images.shape[1:]
        outs = [jax.ShapeDtypeStruct(shape, BF16)] * y_size
        if keeps:
            outs.append(jax.ShapeDtypeStruct((keeps,) + own_images.shape, BF16))
        before = [groups[step - 1][1], groups[step - 1][-1]] if step in (1, 2) else []
        picked = pl.pallas_call(
            functools.partial(pick_kernel, step=step, sizes=sizes, onward=keeps),
            out_shape=outs,
            in_specs=[whole(pltpu.SMEM)] * 2 + [whole()] + [whole(pl.ANY)] * len(before),
            out_specs=[whole(pl.ANY)] * len(outs),
            scratch_shapes=[pltpu.SemaphoreType.DMA((1 + y_size * shape[0],))],
            cost_estimate=pl.CostEstimate(flops=1, bytes_accessed=1, transcendentals=0),
            name="pick",
        )(table, place, here, *before)
        if keeps:
            moving = picked[-1]
        groups.append(
            [picked[0]] + [lax.ppermute(picked[n], "y", shifted(y_size, n)) for n in range(1, y_size)]
        )
    return groups


def solution(mesh):
    x_size = mesh.shape["replica"]
    c_size = 2
    z_size = 2 * x_size
    y_size = mesh.shape["dp"] // (z_size * c_size)
    fine = Mesh(mesh.devices.reshape(z_size, y_size, c_size, x_size), ("z", "y", "c", "x"))
    placed = (P(DP, "x", None, None), P(), P(DP, None, None), P(DP, None), P(), P(), P())
    return jax.shard_map(
        on_device,
        mesh=fine,
        in_specs=placed,
        out_specs=(P(DP, "x"), P("x", DP)),
        check_vma=False,
    )
```

```python
import functools

import jax
import jax.numpy as jnp
from jax import lax
from jax.experimental import pallas as pl
from jax.experimental.pallas import tpu as pltpu
from jax.sharding import Mesh, PartitionSpec as P

EPSILON = 1e-06
DP = ("z", "y", "c")
GROUP = 2
EXTRA = 128
F32 = jnp.float32
BF16 = jnp.bfloat16


def dot(a, b, contract):
    return lax.dot_general(a, b, ((contract[:1], contract[1:]), ((), ())), preferred_element_type=F32)


def unit_rows(values):
    inverse = lax.rsqrt(jnp.sum(values * values, axis=-1, keepdims=True) + EPSILON)
    return (values * inverse, inverse)


def shifted(size, shift):
    return [(i, (i + shift) % size) for i in range(size)]


def loss_and_weight(logits):
    small = jnp.exp(-jnp.abs(logits))
    share = 1.0 / (1.0 + small)
    weight = jnp.where(logits >= 0, share, small * share)
    return (jnp.maximum(logits, 0.0) + jnp.log1p(small), weight)


def project_kernel(features, weight, *refs):
    out, acc = refs[-2:]
    step = pl.program_id(0)

    @pl.when(step == 0)
    def _():
        acc[...] = jnp.zeros_like(acc)

    acc[...] += dot(features[...], weight[...], (1, 0))

    @pl.when(step == pl.num_programs(0) - 1)
    def _():
        unit, inverse = unit_rows(acc[...])
        width = unit.shape[1]
        text = unit.astype(BF16)
        first = inverse.astype(BF16).astype(F32)
        second = (inverse - first).astype(BF16).astype(F32)
        third = inverse - first - second
        lane = lax.broadcasted_iota(jnp.int32, (unit.shape[0], EXTRA), 1)
        terms = jnp.where(lane == 0, first, jnp.where(lane == 1, second, jnp.where(lane == 2, third, 0.0)))
        terms = terms.astype(BF16)
        for k in range(out.shape[0]):
            out[k, :, :width] = text
            out[k, :, width:] = terms


def add_tiles(t, text, acc, sources, slots, counts, scale_bias, arrived, pair_loss):
    scale, bias = scale_bias[0], scale_bias[1]
    piece_rows = arrived.shape[1]
    count = counts[t]

    def each_group(g, carry):
        held = [slots[t, g * GROUP + i] for i in range(GROUP)]
        rows = jnp.concatenate([arrived[held[i]] for i in range(GROUP)], axis=0)
        values = scale * dot(text, rows, (1, 1)) + bias
        terms, shares = loss_and_weight(values)
        sums = jnp.sum(terms, axis=0, keepdims=True)
        left = (count - g * GROUP) * piece_rows
        live = lax.broadcasted_iota(jnp.int32, shares.shape, 1) < left
        shares = jnp.where(live, shares, 0.0).astype(BF16)
        acc[...] += dot(shares, rows, (1, 0))
        for i in range(GROUP):

            @pl.when(g * GROUP + i < count)
            def _():
                source = sources[t, g * GROUP + i]
                pair_loss[pl.ds(source, 1)] = sums[:, i * piece_rows : (i + 1) * piece_rows][None]

        return carry

    lax.fori_loop(0, (count + GROUP - 1) // GROUP, each_group, 0)


def bring(arriving, arrived, starts, sems, half):
    copies = []
    for n, (ref, at) in enumerate(zip(arriving, starts)):
        count = ref.shape[0] // 2
        rows = ref.at[pl.ds(half * count, count)]
        copies.append(pltpu.make_async_copy(rows, arrived.at[pl.ds(at, count)], sems.at[n]))
    return copies


def pair_kernel(sources, slots, counts, place, scale_bias, texts, *refs, starts, own):
    if own:
        own_images, image_docs, text_docs, *refs = refs
    arriving, refs = refs[: len(starts)], refs[len(starts) :]
    chunks, pair_loss, *refs = refs
    if own:
        own_loss, *refs = refs
    acc, arrived, sems = refs
    t = pl.program_id(0)
    quarters, _, _, piece_rows, part = chunks.shape
    width = quarters * part
    copies = bring(arriving, arrived, starts, sems, 0 if own else 1)

    @pl.when(t == 0)
    def _():
        for copy in copies:
            copy.start()
        pair_loss[...] = jnp.zeros_like(pair_loss)

    scale, bias = scale_bias[0], scale_bias[1]
    block = texts[...].reshape(quarters * piece_rows, width + EXTRA)
    text = block[:, :width]
    if own:
        images = own_images[0]
        logits = scale * dot(text, images, (1, 1)) + bias
        same = text_docs[0] == image_docs[0]
        sign = jnp.where(same, 1.0, -1.0)
        loss, weight = loss_and_weight(-sign * logits)
        own_loss[0] = jnp.sum(loss, axis=0, keepdims=True)
        acc[...] = dot((-sign * weight).astype(BF16), images, (1, 0))
    else:
        acc[...] = jnp.zeros_like(acc)

    @pl.when(t == 0)
    def _():
        for copy in copies:
            copy.wait()

    add_tiles(t, text, acc, sources, slots, counts, scale_bias, arrived, pair_loss)
    inverse = jnp.sum(block[:, width:].astype(F32), axis=-1, keepdims=True)
    unit = text.astype(F32)
    grad = scale * acc[...]
    along = jnp.sum(unit * grad, axis=-1, keepdims=True)
    acc[...] = (grad - unit * along) * inverse
    for k in range(quarters):
        start = pl.multiple_of(lax.rem(place[0] + k, quarters) * part, part)
        values = acc[:, pl.ds(start, part)].astype(BF16)
        for j in range(quarters):
            chunks[k, j, 0] = values[j * piece_rows : (j + 1) * piece_rows]


def pick_kernel(table, place, from_ref, *refs, step, sizes, onward):
    z_size, y_size, c_size = sizes
    sems = refs[-1]
    outs = y_size + (onward > 0)
    to_refs = refs[-1 - outs : -1]
    count = from_ref.shape[0]
    back = jnp.where(place[2] == 0, step, z_size - step)
    z = lax.rem(place[3] - back + z_size, z_size)
    copies = []
    if onward:
        copies.append(pltpu.make_async_copy(from_ref.at[pl.ds(0, onward)], to_refs[-1], sems.at[0]))
    for dy in range(y_size):
        y = lax.rem(place[1] + dy, y_size)
        for to in range(c_size):
            for j in range(count):
                source = z * c_size + lax.rem(place[2] + j, c_size)
                block = table[source, y * c_size + lax.rem(place[2] + to, c_size)]
                n = to * count + j
                sem = sems.at[1 + dy * c_size * count + n]
                copies.append(pltpu.make_async_copy(from_ref.at[j, block], to_refs[dy].at[n], sem))
    for copy in copies:
        copy.start()
    for copy in copies:
        copy.wait()


def head_kernel(place, grad_0, grad_1, grad_2, grad_3, feats, first_done, keep, give, turned, *, sizes, strip):
    z_part, y_size, c_size = sizes

    @pl.when(pl.program_id(0) == 0)
    def _():
        total = sum(g[...].astype(F32) for g in (grad_0, grad_1, grad_2, grad_3))
        flipped = total.T.astype(BF16)
        for zz in range(z_part):
            for y in range(y_size):
                for c in range(c_size):
                    block = flipped[((zz * y_size + y) * c_size + c) * strip :][:strip]
                    y_rel = lax.rem(y - place[1] + y_size, y_size)
                    c_rel = lax.rem(c - place[2] + c_size, c_size)
                    to = ((c_rel * y_size + y_rel) * z_part + zz) * strip
                    turned[pl.ds(pl.multiple_of(to, strip), strip)] = block

    half = keep.shape[0]
    total = dot(turned[...], feats[...], (1, 0)).astype(BF16)
    keep[...] = total[:half]
    give[...] = total[half:]


def whole(memory=pltpu.VMEM):
    return pl.BlockSpec(memory_space=memory)


def on_device(
    text_features, head_weight, image_embeds, doc_ids, hard_lists, logit_scale, logit_bias
):
    z_size, y_size, c_size, x_size = (lax.axis_size(name) for name in ("z", "y", "c", "x"))
    z, y, c, x = (lax.axis_index(name) for name in ("z", "y", "c", "x"))
    dp_count = z_size * y_size * c_size
    dp_index = (z * y_size + y) * c_size + c
    blocks, _, piece_rows, feat_width = text_features.shape
    block_rows = image_embeds.shape[1]
    emb_width = head_weight.shape[1]
    rows = blocks * piece_rows
    part = emb_width // x_size
    strip = emb_width // dp_count
    block_iota = jnp.arange(blocks, dtype=jnp.int32)
    peer_iota = jnp.arange(dp_count, dtype=jnp.int32)
    place = jnp.stack([x, y, c, z]).astype(jnp.int32)
    features = text_features.reshape(rows, feat_width)
    feats = lax.all_gather(features, "x", axis=0, tiled=False)

    owners = jnp.where(hard_lists >= 0, hard_lists // blocks, -1).reshape(dp_count, blocks, -1)
    line = owners.reshape(z_size, y_size, c_size, blocks, -1)
    line = lax.dynamic_index_in_dim(line, y, 1, keepdims=False).reshape(z_size * c_size, blocks, -1)
    plane = z * y_size * c_size + jnp.arange(y_size * c_size, dtype=jnp.int32)
    wanted = jnp.any(line[:, None] == plane[:, None, None], axis=3)
    table = jnp.sum(wanted.astype(jnp.int32) * block_iota, axis=2)

    own_images = lax.dynamic_slice_in_dim(image_embeds, x * piece_rows, piece_rows, 1)
    own_images = unit_rows(own_images.astype(F32))[0].astype(BF16)
    tile = min(1024, feat_width)
    project = pl.pallas_call(
        project_kernel,
        grid=(feat_width // tile,),
        out_shape=jax.ShapeDtypeStruct((x_size * c_size, rows, emb_width + EXTRA), BF16),
        in_specs=[
            pl.BlockSpec((rows, tile), lambda i: (0, i)),
            pl.BlockSpec((tile, emb_width), lambda i: (i, 0)),
        ]
        + [whole(pl.ANY)] * (y_size + 1),
        out_specs=pl.BlockSpec((x_size * c_size, rows, emb_width + EXTRA), lambda i: (0, 0, 0)),
        scratch_shapes=[pltpu.VMEM((rows, emb_width), F32)],
        compiler_params=pltpu.CompilerParams(vmem_limit_bytes=60 << 20),
        cost_estimate=pl.CostEstimate(flops=1, bytes_accessed=1, transcendentals=0),
        name="project",
    )
    groups, text_emb = exchange_images(
        own_images,
        table,
        place,
        (z_size, y_size, c_size),
        lambda *first: project(features, head_weight, *first),
    )

    texts = lax.all_to_all(text_emb, ("x", "c"), split_axis=0, concat_axis=0, tiled=True)
    texts = texts.reshape(x_size, c_size, rows, emb_width + EXTRA)

    arrays, starts, slot_base, turns = [], [], [], 0
    for group in groups:
        count = group[0].shape[0] // c_size
        slot_base.append(turns)
        for array in group:
            arrays.append(array)
            starts.append(turns)
            turns += count
    away = jnp.where(c == 0, z - peer_iota // (y_size * c_size), peer_iota // (y_size * c_size) - z) % z_size
    over_y = (y - peer_iota // c_size) % y_size
    over_c = (c - peer_iota) % c_size
    ends = (away == 0) | (away == z_size // 2)
    have = jnp.where(ends, over_c == 0, away < z_size // 2)
    base = sum(jnp.where(away == k, b, 0) for k, b in enumerate(slot_base))
    slot_of = base + jnp.where(ends, over_y, over_y * c_size + over_c)

    text_docs = doc_ids.reshape(blocks, block_rows, 1)
    image_docs = lax.dynamic_slice_in_dim(doc_ids, x * piece_rows, piece_rows, 1)[:, None]
    scale_bias = jnp.stack([logit_scale, logit_bias])

    def lists(holder, here):
        hit = owners == holder
        which = jnp.sum(hit * (hard_lists % blocks).reshape(owners.shape), axis=(1, 2))
        mine = (jnp.any(hit, axis=(1, 2)) & here)[None] & (which[None] == block_iota[:, None])
        before = peer_iota[None] < peer_iota[:, None]
        order = jnp.sum((mine[:, None] & before).astype(jnp.int32), axis=2)
        at = mine[:, None] & (order[:, None] == peer_iota[:, None])
        sources = jnp.sum(jnp.where(at, peer_iota, 0), axis=2)
        return sources, jnp.sum(jnp.where(at, slot_of, 0), axis=2), jnp.sum(mine.astype(jnp.int32), axis=1)

    loss_shape = jax.ShapeDtypeStruct((dp_count, 1, piece_rows), F32)

    def pairs(holder, pieces, own):
        extra, extra_specs, losses, loss_specs = [], [], [], []
        if own:
            extra = [own_images, image_docs, text_docs]
            extra_specs = [pl.BlockSpec((1,) + v.shape[1:], lambda t: (t, 0, 0)) for v in extra]
            losses = [jax.ShapeDtypeStruct((blocks, 1, piece_rows), F32)]
            loss_specs = [pl.BlockSpec((1, 1, piece_rows), lambda t: (t, 0, 0))]
        return pl.pallas_call(
            functools.partial(pair_kernel, starts=starts, own=own),
            grid=(blocks,),
            out_shape=[
                jax.ShapeDtypeStruct((x_size, x_size, blocks, piece_rows, part), BF16),
                loss_shape,
            ]
            + losses,
            in_specs=[whole(pltpu.SMEM)] * 5
            + [pl.BlockSpec((x_size, 1, piece_rows, emb_width + EXTRA), lambda t: (0, t, 0, 0))]
            + extra_specs
            + [whole(pl.ANY)] * len(arrays),
            out_specs=[
                pl.BlockSpec((x_size, x_size, 1, piece_rows, part), lambda t: (0, 0, t, 0, 0)),
                pl.BlockSpec(loss_shape.shape, lambda t: (0, 0, 0)),
            ]
            + loss_specs,
            scratch_shapes=[
                pltpu.VMEM((block_rows, emb_width), F32),
                pltpu.VMEM((turns, piece_rows, emb_width), BF16),
                pltpu.SemaphoreType.DMA((len(arrays),)),
            ],
            compiler_params=pltpu.CompilerParams(vmem_limit_bytes=60 << 20),
            cost_estimate=pl.CostEstimate(flops=1, bytes_accessed=1, transcendentals=0),
            name="pairs",
        )(
            *lists(holder, have),
            place,
            scale_bias,
            pieces.reshape(x_size, blocks, piece_rows, emb_width + EXTRA),
            *extra,
            *arrays,
        )

    other_texts = lax.dynamic_index_in_dim(texts, 1 - c, 1, keepdims=False)
    other_chunks, other_loss = pairs(dp_index + 1 - 2 * c, other_texts, False)
    own_texts = lax.dynamic_index_in_dim(texts, c, 1, keepdims=False)
    chunks, pair_loss, own_loss = pairs(dp_index, own_texts, True)

    returned = lax.all_to_all(
        jnp.concatenate([pair_loss, other_loss], axis=1), DP, split_axis=0, concat_axis=0, tiled=True
    )

    taken = lax.ppermute(other_chunks, "c", shifted(c_size, 1))
    grads = []
    for k in range(x_size):
        total = (chunks[k].astype(F32) + taken[k].astype(F32)).astype(BF16).reshape(x_size * rows, part)
        grads.append(lax.ppermute(total, "x", shifted(x_size, k)) if k else total)
    z_part = z_size // x_size
    half = part // c_size
    keep, give = pl.pallas_call(
        functools.partial(head_kernel, sizes=(z_part, y_size, c_size), strip=strip),
        grid=(feat_width // tile,),
        out_shape=(
            jax.ShapeDtypeStruct((half, feat_width), BF16),
            jax.ShapeDtypeStruct((half, feat_width), BF16),
        ),
        in_specs=[whole(pltpu.SMEM)]
        + [whole()] * 4
        + [pl.BlockSpec((x_size * rows, tile), lambda i: (0, i)), whole(pl.ANY)],
        out_specs=(
            pl.BlockSpec((half, tile), lambda i: (0, i)),
            pl.BlockSpec((half, tile), lambda i: (0, i)),
        ),
        scratch_shapes=[pltpu.VMEM((part, x_size * rows), BF16)],
        compiler_params=pltpu.CompilerParams(vmem_limit_bytes=60 << 20),
        cost_estimate=pl.CostEstimate(
            flops=2 * rows * feat_width * emb_width, bytes_accessed=16 << 20, transcendentals=0
        ),
        name="head",
    )(place, *grads, feats.reshape(x_size * rows, feat_width), returned)

    swapped = returned.reshape(-1, c_size, 2, piece_rows)[:, ::-1, 1].reshape(dp_count, piece_rows)
    returned = returned[:, 0] + swapped
    my_owners = lax.dynamic_index_in_dim(owners, dp_index, 0, keepdims=False)
    asked = jnp.any(my_owners[None] == peer_iota[:, None, None], axis=2)
    remote_loss = jnp.sum(jnp.where(asked[..., None], returned[:, None], 0.0), axis=0)
    row_loss = (own_loss.reshape(blocks, piece_rows) + remote_loss) / block_rows
    return (row_loss, add_over_dp(keep, give, (z_size, y_size, c_size, x_size), z, strip))


def add_over_dp(keep, give, sizes, z, strip):
    z_size, y_size, c_size, x_size = sizes
    z_part = z_size // x_size
    width = keep.shape[1]

    def add(*values):
        return sum(v.astype(F32) for v in values).astype(BF16)

    total = add(keep, lax.ppermute(give, "c", shifted(c_size, 1)))
    total = total.reshape(y_size, z_part * strip, width)
    total = add(
        total[0], *(lax.ppermute(total[k], "y", shifted(y_size, k)) for k in range(1, y_size))
    ).reshape(z_part, strip, width)
    low, top = z % 2, z // (z_size // 2)
    given = lax.dynamic_index_in_dim(total, 1 - low, 0, keepdims=False)
    kept = lax.dynamic_index_in_dim(total, low, 0, keepdims=False)
    total = add(kept, lax.ppermute(given, "z", [(i, i ^ 1) for i in range(z_size)]))
    total = total.reshape(strip, 2, width // 2)
    given = lax.dynamic_index_in_dim(total, 1 - top, 1, keepdims=False)
    kept = lax.dynamic_index_in_dim(total, top, 1, keepdims=False)
    total = add(kept, lax.ppermute(given, "z", [(i, (i + z_size // 2) % z_size) for i in range(z_size)]))
    total = total.reshape(strip, 2, width // 4)
    final = 0.0
    for flip in range(2):
        pairs = []
        for z_from in range(z_size):
            bit = (z_from // 2 % 2) ^ flip
            for x_from in range(x_size):
                to_z, to_x = z_part * x_from + z_from % 2, z_from // (z_size // 2) * 2 + bit
                pairs.append((z_from * x_size + x_from, to_z * x_size + to_x))
        chunk = lax.dynamic_index_in_dim(total, (z // 2 % 2) ^ flip, 1, keepdims=False)
        final = final + lax.ppermute(chunk, ("z", "x"), pairs).astype(F32)
    return final.T


def exchange_images(own_images, table, place, sizes, project):
    z_size, y_size, c_size = sizes
    onward = []
    for z in range(z_size):
        onward.append((z * c_size, (z + 1) % z_size * c_size))
        onward.append((z * c_size + 1, (z - 1) % z_size * c_size + 1))
    moving = jnp.stack([own_images, lax.ppermute(own_images, "c", shifted(c_size, 1))])
    groups = []
    last = z_size // 2
    for step in range(last + 1):
        here = own_images[None] if step == 0 else lax.ppermute(moving, ("z", "c"), onward)
        keeps = 0 if step in (0, last) else 1 if step == last - 1 else c_size
        shape = (c_size * here.shape[0],) + own_images.shape[1:]
        outs = [jax.ShapeDtypeStruct(shape, BF16)] * y_size
        if keeps:
            outs.append(jax.ShapeDtypeStruct((keeps,) + own_images.shape, BF16))
        before = [groups[step - 1][1], groups[step - 1][-1]] if step in (1, 2) else []
        if step == 1:
            text_emb = project(*groups[0], here)
        picked = pl.pallas_call(
            functools.partial(pick_kernel, step=step, sizes=sizes, onward=keeps),
            out_shape=outs,
            in_specs=[whole(pltpu.SMEM)] * 2 + [whole()] + [whole(pl.ANY)] * len(before),
            out_specs=[whole(pl.ANY)] * len(outs),
            scratch_shapes=[pltpu.SemaphoreType.DMA((1 + y_size * shape[0],))],
            cost_estimate=pl.CostEstimate(flops=1, bytes_accessed=1, transcendentals=0),
            name="pick",
        )(table, place, here, *before)
        if keeps:
            moving = picked[-1]
        groups.append(
            [picked[0]] + [lax.ppermute(picked[n], "y", shifted(y_size, n)) for n in range(1, y_size)]
        )
    return groups, text_emb


def solution(mesh):
    x_size = mesh.shape["replica"]
    c_size = 2
    z_size = 2 * x_size
    y_size = mesh.shape["dp"] // (z_size * c_size)
    fine = Mesh(mesh.devices.reshape(z_size, y_size, c_size, x_size), ("z", "y", "c", "x"))
    placed = (P(DP, "x", None, None), P(), P(DP, None, None), P(DP, None), P(), P(), P())
    return jax.shard_map(
        on_device,
        mesh=fine,
        in_specs=placed,
        out_specs=(P(DP, "x"), P("x", DP)),
        check_vma=False,
    )
```

```python
import functools

import jax
import jax.numpy as jnp
from jax import lax
from jax.experimental import pallas as pl
from jax.experimental.pallas import tpu as pltpu
from jax.sharding import Mesh, PartitionSpec as P

EPSILON = 1e-06
DP = ("z", "y", "c")
GROUP = 2
EXTRA = 128
F32 = jnp.float32
BF16 = jnp.bfloat16


def dot(a, b, contract):
    return lax.dot_general(a, b, ((contract[:1], contract[1:]), ((), ())), preferred_element_type=F32)


def unit_rows(values):
    inverse = lax.rsqrt(jnp.sum(values * values, axis=-1, keepdims=True) + EPSILON)
    return (values * inverse, inverse)


def shifted(size, shift):
    return [(i, (i + shift) % size) for i in range(size)]


def loss_and_weight(logits):
    small = jnp.exp(-jnp.abs(logits))
    share = 1.0 / (1.0 + small)
    weight = jnp.where(logits >= 0, share, small * share)
    return (jnp.maximum(logits, 0.0) + jnp.log1p(small), weight)


def project_kernel(features, weight, *refs):
    out, acc = refs[-2:]
    step = pl.program_id(0)

    @pl.when(step == 0)
    def _():
        acc[...] = jnp.zeros_like(acc)

    acc[...] += dot(features[...], weight[...], (1, 0))

    @pl.when(step == pl.num_programs(0) - 1)
    def _():
        unit, inverse = unit_rows(acc[...])
        width = unit.shape[1]
        text = unit.astype(BF16)
        first = inverse.astype(BF16).astype(F32)
        second = (inverse - first).astype(BF16).astype(F32)
        third = inverse - first - second
        lane = lax.broadcasted_iota(jnp.int32, (unit.shape[0], EXTRA), 1)
        terms = jnp.where(lane == 0, first, jnp.where(lane == 1, second, jnp.where(lane == 2, third, 0.0)))
        terms = terms.astype(BF16)
        for k in range(out.shape[0]):
            out[k, :, :width] = text
            out[k, :, width:] = terms


def add_tiles(t, text, acc, sources, slots, counts, scale_bias, arrived, pair_loss):
    scale, bias = scale_bias[0], scale_bias[1]
    piece_rows = arrived.shape[1]
    count = counts[t]

    def each_group(g, carry):
        held = [slots[t, g * GROUP + i] for i in range(GROUP)]
        rows = jnp.concatenate([arrived[held[i]] for i in range(GROUP)], axis=0)
        values = scale * dot(text, rows, (1, 1)) + bias
        terms, shares = loss_and_weight(values)
        sums = jnp.sum(terms, axis=0, keepdims=True)
        left = (count - g * GROUP) * piece_rows
        live = lax.broadcasted_iota(jnp.int32, shares.shape, 1) < left
        shares = jnp.where(live, shares, 0.0).astype(BF16)
        acc[...] += dot(shares, rows, (1, 0))
        for i in range(GROUP):

            @pl.when(g * GROUP + i < count)
            def _():
                source = sources[t, g * GROUP + i]
                pair_loss[pl.ds(source, 1)] = sums[:, i * piece_rows : (i + 1) * piece_rows][None]

        return carry

    lax.fori_loop(0, (count + GROUP - 1) // GROUP, each_group, 0)


def bring(arriving, arrived, starts, sems, half):
    copies = []
    for n, (ref, at) in enumerate(zip(arriving, starts)):
        count = ref.shape[0] // 2
        rows = ref.at[pl.ds(half * count, count)]
        copies.append(pltpu.make_async_copy(rows, arrived.at[pl.ds(at, count)], sems.at[n]))
    return copies


def pair_kernel(sources, slots, counts, place, scale_bias, texts, *refs, starts, own):
    if own:
        own_images, image_docs, text_docs, *refs = refs
    arriving, refs = refs[: len(starts)], refs[len(starts) :]
    chunks, pair_loss, *refs = refs
    if own:
        own_loss, *refs = refs
    acc, arrived, sems = refs
    t = pl.program_id(0)
    quarters, _, _, piece_rows, part = chunks.shape
    width = quarters * part
    copies = bring(arriving, arrived, starts, sems, 0 if own else 1)

    @pl.when(t == 0)
    def _():
        for copy in copies:
            copy.start()
        pair_loss[...] = jnp.zeros_like(pair_loss)

    scale, bias = scale_bias[0], scale_bias[1]
    block = texts[...].reshape(quarters * piece_rows, width + EXTRA)
    text = block[:, :width]
    if own:
        images = own_images[0]
        logits = scale * dot(text, images, (1, 1)) + bias
        same = text_docs[0] == image_docs[0]
        sign = jnp.where(same, 1.0, -1.0)
        loss, weight = loss_and_weight(-sign * logits)
        own_loss[0] = jnp.sum(loss, axis=0, keepdims=True)
        acc[...] = dot((-sign * weight).astype(BF16), images, (1, 0))
    else:
        acc[...] = jnp.zeros_like(acc)

    @pl.when(t == 0)
    def _():
        for copy in copies:
            copy.wait()

    add_tiles(t, text, acc, sources, slots, counts, scale_bias, arrived, pair_loss)
    inverse = jnp.sum(block[:, width:].astype(F32), axis=-1, keepdims=True)
    unit = text.astype(F32)
    grad = scale * acc[...]
    along = jnp.sum(unit * grad, axis=-1, keepdims=True)
    acc[...] = (grad - unit * along) * inverse
    for k in range(quarters):
        start = pl.multiple_of(lax.rem(place[0] + k, quarters) * part, part)
        values = acc[:, pl.ds(start, part)].astype(BF16)
        for j in range(quarters):
            chunks[k, j, 0] = values[j * piece_rows : (j + 1) * piece_rows]


def pick_kernel(table, place, from_ref, *refs, step, sizes, onward, carries):
    z_size, y_size, c_size = sizes
    sems = refs[-1]
    outs = y_size + (onward > 0) + carries
    to_refs = refs[-1 - outs : -1]
    count = from_ref.shape[0]
    back = jnp.where(place[2] == 0, step, z_size - step)
    z = lax.rem(place[3] - back + z_size, z_size)
    copies = []
    if onward:
        copies.append(pltpu.make_async_copy(from_ref.at[pl.ds(0, onward)], to_refs[y_size], sems.at[0]))
    if carries:
        copies.append(pltpu.make_async_copy(refs[0], to_refs[-1], sems.at[1]))
    for dy in range(y_size):
        y = lax.rem(place[1] + dy, y_size)
        for to in range(c_size):
            for j in range(count):
                source = z * c_size + lax.rem(place[2] + j, c_size)
                block = table[source, y * c_size + lax.rem(place[2] + to, c_size)]
                n = to * count + j
                sem = sems.at[2 + dy * c_size * count + n]
                copies.append(pltpu.make_async_copy(from_ref.at[j, block], to_refs[dy].at[n], sem))
    for copy in copies:
        copy.start()
    for copy in copies:
        copy.wait()


def head_kernel(place, grad_0, grad_1, grad_2, grad_3, feats, first_done, keep, give, turned, *, sizes, strip):
    z_part, y_size, c_size = sizes

    @pl.when(pl.program_id(0) == 0)
    def _():
        total = sum(g[...].astype(F32) for g in (grad_0, grad_1, grad_2, grad_3))
        flipped = total.T.astype(BF16)
        for zz in range(z_part):
            for y in range(y_size):
                for c in range(c_size):
                    block = flipped[((zz * y_size + y) * c_size + c) * strip :][:strip]
                    y_rel = lax.rem(y - place[1] + y_size, y_size)
                    c_rel = lax.rem(c - place[2] + c_size, c_size)
                    to = ((c_rel * y_size + y_rel) * z_part + zz) * strip
                    turned[pl.ds(pl.multiple_of(to, strip), strip)] = block

    half = keep.shape[0]
    total = dot(turned[...], feats[...], (1, 0)).astype(BF16)
    keep[...] = total[:half]
    give[...] = total[half:]


def whole(memory=pltpu.VMEM):
    return pl.BlockSpec(memory_space=memory)


def on_device(
    text_features, head_weight, image_embeds, doc_ids, hard_lists, logit_scale, logit_bias
):
    z_size, y_size, c_size, x_size = (lax.axis_size(name) for name in ("z", "y", "c", "x"))
    z, y, c, x = (lax.axis_index(name) for name in ("z", "y", "c", "x"))
    dp_count = z_size * y_size * c_size
    dp_index = (z * y_size + y) * c_size + c
    blocks, _, piece_rows, feat_width = text_features.shape
    block_rows = image_embeds.shape[1]
    emb_width = head_weight.shape[1]
    rows = blocks * piece_rows
    part = emb_width // x_size
    strip = emb_width // dp_count
    block_iota = jnp.arange(blocks, dtype=jnp.int32)
    peer_iota = jnp.arange(dp_count, dtype=jnp.int32)
    place = jnp.stack([x, y, c, z]).astype(jnp.int32)
    features = text_features.reshape(rows, feat_width)

    owners = jnp.where(hard_lists >= 0, hard_lists // blocks, -1).reshape(dp_count, blocks, -1)
    line = owners.reshape(z_size, y_size, c_size, blocks, -1)
    line = lax.dynamic_index_in_dim(line, y, 1, keepdims=False).reshape(z_size * c_size, blocks, -1)
    plane = z * y_size * c_size + jnp.arange(y_size * c_size, dtype=jnp.int32)
    wanted = jnp.any(line[:, None] == plane[:, None, None], axis=3)
    table = jnp.sum(wanted.astype(jnp.int32) * block_iota, axis=2)

    own_images = lax.dynamic_slice_in_dim(image_embeds, x * piece_rows, piece_rows, 1)
    own_images = unit_rows(own_images.astype(F32))[0].astype(BF16)
    tile = min(1024, feat_width)
    project = pl.pallas_call(
        project_kernel,
        grid=(feat_width // tile,),
        out_shape=jax.ShapeDtypeStruct((x_size, rows, emb_width + EXTRA), BF16),
        in_specs=[
            pl.BlockSpec((rows, tile), lambda i: (0, i)),
            pl.BlockSpec((tile, emb_width), lambda i: (i, 0)),
        ]
        + [whole(pl.ANY)] * 2,
        out_specs=pl.BlockSpec((x_size, rows, emb_width + EXTRA), lambda i: (0, 0, 0)),
        scratch_shapes=[pltpu.VMEM((rows, emb_width), F32)],
        compiler_params=pltpu.CompilerParams(vmem_limit_bytes=60 << 20),
        cost_estimate=pl.CostEstimate(flops=1, bytes_accessed=1, transcendentals=0),
        name="project",
    )
    groups, texts, sent_features = exchange_images(
        own_images,
        table,
        place,
        (z_size, y_size, c_size),
        lambda *first: project(features, head_weight, *first),
        features,
    )
    feats = lax.all_gather(sent_features, "x", axis=0, tiled=False)

    arrays, starts, slot_base, turns = [], [], [], 0
    for group in groups:
        count = group[0].shape[0] // c_size
        slot_base.append(turns)
        for array in group:
            arrays.append(array)
            starts.append(turns)
            turns += count
    away = jnp.where(c == 0, z - peer_iota // (y_size * c_size), peer_iota // (y_size * c_size) - z) % z_size
    over_y = (y - peer_iota // c_size) % y_size
    over_c = (c - peer_iota) % c_size
    ends = (away == 0) | (away == z_size // 2)
    have = jnp.where(ends, over_c == 0, away < z_size // 2)
    base = sum(jnp.where(away == k, b, 0) for k, b in enumerate(slot_base))
    slot_of = base + jnp.where(ends, over_y, over_y * c_size + over_c)

    text_docs = doc_ids.reshape(blocks, block_rows, 1)
    image_docs = lax.dynamic_slice_in_dim(doc_ids, x * piece_rows, piece_rows, 1)[:, None]
    scale_bias = jnp.stack([logit_scale, logit_bias])

    def lists(holder, here):
        hit = owners == holder
        which = jnp.sum(hit * (hard_lists % blocks).reshape(owners.shape), axis=(1, 2))
        mine = (jnp.any(hit, axis=(1, 2)) & here)[None] & (which[None] == block_iota[:, None])
        before = peer_iota[None] < peer_iota[:, None]
        order = jnp.sum((mine[:, None] & before).astype(jnp.int32), axis=2)
        at = mine[:, None] & (order[:, None] == peer_iota[:, None])
        sources = jnp.sum(jnp.where(at, peer_iota, 0), axis=2)
        return sources, jnp.sum(jnp.where(at, slot_of, 0), axis=2), jnp.sum(mine.astype(jnp.int32), axis=1)

    loss_shape = jax.ShapeDtypeStruct((dp_count, 1, piece_rows), F32)

    def pairs(holder, pieces, own):
        extra, extra_specs, losses, loss_specs = [], [], [], []
        if own:
            extra = [own_images, image_docs, text_docs]
            extra_specs = [pl.BlockSpec((1,) + v.shape[1:], lambda t: (t, 0, 0)) for v in extra]
            losses = [jax.ShapeDtypeStruct((blocks, 1, piece_rows), F32)]
            loss_specs = [pl.BlockSpec((1, 1, piece_rows), lambda t: (t, 0, 0))]
        return pl.pallas_call(
            functools.partial(pair_kernel, starts=starts, own=own),
            grid=(blocks,),
            out_shape=[
                jax.ShapeDtypeStruct((x_size, x_size, blocks, piece_rows, part), BF16),
                loss_shape,
            ]
            + losses,
            in_specs=[whole(pltpu.SMEM)] * 5
            + [pl.BlockSpec((x_size, 1, piece_rows, emb_width + EXTRA), lambda t: (0, t, 0, 0))]
            + extra_specs
            + [whole(pl.ANY)] * len(arrays),
            out_specs=[
                pl.BlockSpec((x_size, x_size, 1, piece_rows, part), lambda t: (0, 0, t, 0, 0)),
                pl.BlockSpec(loss_shape.shape, lambda t: (0, 0, 0)),
            ]
            + loss_specs,
            scratch_shapes=[
                pltpu.VMEM((block_rows, emb_width), F32),
                pltpu.VMEM((turns, piece_rows, emb_width), BF16),
                pltpu.SemaphoreType.DMA((len(arrays),)),
            ],
            compiler_params=pltpu.CompilerParams(vmem_limit_bytes=60 << 20),
            cost_estimate=pl.CostEstimate(flops=1, bytes_accessed=1, transcendentals=0),
            name="pairs",
        )(
            *lists(holder, have),
            place,
            scale_bias,
            pieces.reshape(x_size, blocks, piece_rows, emb_width + EXTRA),
            *extra,
            *arrays,
        )

    other_texts = lax.ppermute(texts, "c", shifted(c_size, 1))
    other_chunks, other_loss = pairs(dp_index + 1 - 2 * c, other_texts, False)
    chunks, pair_loss, own_loss = pairs(dp_index, texts, True)

    returned = lax.all_to_all(
        jnp.concatenate([pair_loss, other_loss], axis=1), DP, split_axis=0, concat_axis=0, tiled=True
    )

    taken = lax.ppermute(other_chunks, "c", shifted(c_size, 1))
    grads = []
    for k in range(x_size):
        total = (chunks[k].astype(F32) + taken[k].astype(F32)).astype(BF16).reshape(x_size * rows, part)
        grads.append(lax.ppermute(total, "x", shifted(x_size, k)) if k else total)
    z_part = z_size // x_size
    half = part // c_size
    keep, give = pl.pallas_call(
        functools.partial(head_kernel, sizes=(z_part, y_size, c_size), strip=strip),
        grid=(feat_width // tile,),
        out_shape=(
            jax.ShapeDtypeStruct((half, feat_width), BF16),
            jax.ShapeDtypeStruct((half, feat_width), BF16),
        ),
        in_specs=[whole(pltpu.SMEM)]
        + [whole()] * 4
        + [pl.BlockSpec((x_size * rows, tile), lambda i: (0, i)), whole(pl.ANY)],
        out_specs=(
            pl.BlockSpec((half, tile), lambda i: (0, i)),
            pl.BlockSpec((half, tile), lambda i: (0, i)),
        ),
        scratch_shapes=[pltpu.VMEM((part, x_size * rows), BF16)],
        compiler_params=pltpu.CompilerParams(vmem_limit_bytes=60 << 20),
        cost_estimate=pl.CostEstimate(
            flops=2 * rows * feat_width * emb_width, bytes_accessed=16 << 20, transcendentals=0
        ),
        name="head",
    )(place, *grads, feats.reshape(x_size * rows, feat_width), returned)

    swapped = returned.reshape(-1, c_size, 2, piece_rows)[:, ::-1, 1].reshape(dp_count, piece_rows)
    returned = returned[:, 0] + swapped
    my_owners = lax.dynamic_index_in_dim(owners, dp_index, 0, keepdims=False)
    asked = jnp.any(my_owners[None] == peer_iota[:, None, None], axis=2)
    remote_loss = jnp.sum(jnp.where(asked[..., None], returned[:, None], 0.0), axis=0)
    row_loss = (own_loss.reshape(blocks, piece_rows) + remote_loss) / block_rows
    return (row_loss, add_over_dp(keep, give, (z_size, y_size, c_size, x_size), z, strip))


def add_over_dp(keep, give, sizes, z, strip):
    z_size, y_size, c_size, x_size = sizes
    z_part = z_size // x_size
    width = keep.shape[1]

    def add(*values):
        return sum(v.astype(F32) for v in values).astype(BF16)

    total = add(keep, lax.ppermute(give, "c", shifted(c_size, 1)))
    total = total.reshape(y_size, z_part * strip, width)
    total = add(
        total[0], *(lax.ppermute(total[k], "y", shifted(y_size, k)) for k in range(1, y_size))
    ).reshape(z_part, strip, width)
    low, top = z % 2, z // (z_size // 2)
    given = lax.dynamic_index_in_dim(total, 1 - low, 0, keepdims=False)
    kept = lax.dynamic_index_in_dim(total, low, 0, keepdims=False)
    total = add(kept, lax.ppermute(given, "z", [(i, i ^ 1) for i in range(z_size)]))
    total = total.reshape(strip, 2, width // 2)
    given = lax.dynamic_index_in_dim(total, 1 - top, 1, keepdims=False)
    kept = lax.dynamic_index_in_dim(total, top, 1, keepdims=False)
    total = add(kept, lax.ppermute(given, "z", [(i, (i + z_size // 2) % z_size) for i in range(z_size)]))
    total = total.reshape(strip, 2, width // 4)
    final = 0.0
    for flip in range(2):
        pairs = []
        for z_from in range(z_size):
            bit = (z_from // 2 % 2) ^ flip
            for x_from in range(x_size):
                to_z, to_x = z_part * x_from + z_from % 2, z_from // (z_size // 2) * 2 + bit
                pairs.append((z_from * x_size + x_from, to_z * x_size + to_x))
        chunk = lax.dynamic_index_in_dim(total, (z // 2 % 2) ^ flip, 1, keepdims=False)
        final = final + lax.ppermute(chunk, ("z", "x"), pairs).astype(F32)
    return final.T


def exchange_images(own_images, table, place, sizes, project, features):
    z_size, y_size, c_size = sizes
    onward = []
    for z in range(z_size):
        onward.append((z * c_size, (z + 1) % z_size * c_size))
        onward.append((z * c_size + 1, (z - 1) % z_size * c_size + 1))
    moving = jnp.stack([own_images, lax.ppermute(own_images, "c", shifted(c_size, 1))])
    groups = []
    last = z_size // 2
    for step in range(last + 1):
        here = own_images[None] if step == 0 else lax.ppermute(moving, ("z", "c"), onward)
        keeps = 0 if step in (0, last) else 1 if step == last - 1 else c_size
        shape = (c_size * here.shape[0],) + own_images.shape[1:]
        outs = [jax.ShapeDtypeStruct(shape, BF16)] * y_size
        if keeps:
            outs.append(jax.ShapeDtypeStruct((keeps,) + own_images.shape, BF16))
        before = [groups[step - 1][1], groups[step - 1][-1]] if step else []
        if step == last - 1:
            before.append(groups[0][y_size // 2])
        if step == last:
            before += [groups[k][y_size // 2] for k in range(1, last - 1)]
        if step == 1:
            text_emb = project(here, picked[0])
            texts = lax.all_to_all(text_emb, "x", split_axis=0, concat_axis=0, tiled=True)
        elif step == 2:
            before.append(text_emb)
        carried = [features] if step == 2 else [texts] if step == last else []
        if carried:
            outs.append(jax.ShapeDtypeStruct(carried[0].shape, carried[0].dtype))
        picked = pl.pallas_call(
            functools.partial(pick_kernel, step=step, sizes=sizes, onward=keeps, carries=len(carried)),
            out_shape=outs,
            in_specs=[whole(pltpu.SMEM)] * 2 + [whole()] * (1 + len(carried)) + [whole(pl.ANY)] * len(before),
            out_specs=[whole(pl.ANY)] * len(outs),
            scratch_shapes=[pltpu.SemaphoreType.DMA((2 + y_size * shape[0],))],
            cost_estimate=pl.CostEstimate(flops=1, bytes_accessed=1, transcendentals=0),
            name="pick",
        )(table, place, here, *carried, *before)
        if keeps:
            moving = picked[y_size]
        if step == 2:
            features = picked[-1]
        if step == last:
            texts = picked[-1]
        groups.append(
            [picked[0]] + [lax.ppermute(picked[n], "y", shifted(y_size, n)) for n in range(1, y_size)]
        )
    return groups, texts, features


def solution(mesh):
    x_size = mesh.shape["replica"]
    c_size = 2
    z_size = 2 * x_size
    y_size = mesh.shape["dp"] // (z_size * c_size)
    fine = Mesh(mesh.devices.reshape(z_size, y_size, c_size, x_size), ("z", "y", "c", "x"))
    placed = (P(DP, "x", None, None), P(), P(DP, None, None), P(DP, None), P(), P(), P())
    return jax.shard_map(
        on_device,
        mesh=fine,
        in_specs=placed,
        out_specs=(P(DP, "x"), P("x", DP)),
        check_vma=False,
    )
```

```python
import functools

import jax
import jax.numpy as jnp
from jax import lax
from jax.experimental import pallas as pl
from jax.experimental.pallas import tpu as pltpu
from jax.sharding import Mesh, PartitionSpec as P

EPSILON = 1e-06
DP = ("z", "y", "c")
GROUP = 2
EXTRA = 128
F32 = jnp.float32
BF16 = jnp.bfloat16


def dot(a, b, contract):
    return lax.dot_general(a, b, ((contract[:1], contract[1:]), ((), ())), preferred_element_type=F32)


def unit_rows(values):
    inverse = lax.rsqrt(jnp.sum(values * values, axis=-1, keepdims=True) + EPSILON)
    return (values * inverse, inverse)


def shifted(size, shift):
    return [(i, (i + shift) % size) for i in range(size)]


def loss_and_weight(logits):
    small = jnp.exp(-jnp.abs(logits))
    share = 1.0 / (1.0 + small)
    weight = jnp.where(logits >= 0, share, small * share)
    return (jnp.maximum(logits, 0.0) + jnp.log1p(small), weight)


def project_kernel(features, weight, *refs):
    out, acc = refs[-2:]
    step = pl.program_id(0)

    @pl.when(step == 0)
    def _():
        acc[...] = jnp.zeros_like(acc)

    acc[...] += dot(features[...], weight[...], (1, 0))

    @pl.when(step == pl.num_programs(0) - 1)
    def _():
        unit, inverse = unit_rows(acc[...])
        width = unit.shape[1]
        text = unit.astype(BF16)
        first = inverse.astype(BF16).astype(F32)
        second = (inverse - first).astype(BF16).astype(F32)
        third = inverse - first - second
        lane = lax.broadcasted_iota(jnp.int32, (unit.shape[0], EXTRA), 1)
        terms = jnp.where(lane == 0, first, jnp.where(lane == 1, second, jnp.where(lane == 2, third, 0.0)))
        terms = terms.astype(BF16)
        for k in range(out.shape[0]):
            out[k, :, :width] = text
            out[k, :, width:] = terms


def add_tiles(t, text, acc, sources, slots, counts, scale_bias, arrived, pair_loss):
    scale, bias = scale_bias[0], scale_bias[1]
    piece_rows = arrived.shape[1]
    count = counts[t]

    def each_group(g, carry):
        held = [slots[t, g * GROUP + i] for i in range(GROUP)]
        rows = jnp.concatenate([arrived[held[i]] for i in range(GROUP)], axis=0)
        values = scale * dot(text, rows, (1, 1)) + bias
        terms, shares = loss_and_weight(values)
        sums = jnp.sum(terms, axis=0, keepdims=True)
        left = (count - g * GROUP) * piece_rows
        live = lax.broadcasted_iota(jnp.int32, shares.shape, 1) < left
        shares = jnp.where(live, shares, 0.0).astype(BF16)
        acc[...] += dot(shares, rows, (1, 0))
        for i in range(GROUP):

            @pl.when(g * GROUP + i < count)
            def _():
                source = sources[t, g * GROUP + i]
                pair_loss[pl.ds(source, 1)] = sums[:, i * piece_rows : (i + 1) * piece_rows][None]

        return carry

    lax.fori_loop(0, (count + GROUP - 1) // GROUP, each_group, 0)


def bring(arriving, arrived, starts, sems, half):
    copies = []
    for n, (ref, at) in enumerate(zip(arriving, starts)):
        count = ref.shape[0] // 2
        rows = ref.at[pl.ds(half * count, count)]
        copies.append(pltpu.make_async_copy(rows, arrived.at[pl.ds(at, count)], sems.at[n]))
    return copies


def pair_kernel(sources, slots, counts, place, scale_bias, texts, *refs, starts, own):
    if own:
        own_images, image_docs, text_docs, *refs = refs
    arriving, refs = refs[: len(starts)], refs[len(starts) :]
    chunks, pair_loss, *refs = refs
    if own:
        own_loss, *refs = refs
    acc, arrived, sems = refs
    t = pl.program_id(0)
    quarters, _, _, piece_rows, part = chunks.shape
    width = quarters * part
    copies = bring(arriving, arrived, starts, sems, 0 if own else 1)

    @pl.when(t == 0)
    def _():
        for copy in copies:
            copy.start()
        pair_loss[...] = jnp.zeros_like(pair_loss)

    scale, bias = scale_bias[0], scale_bias[1]
    block = texts[...].reshape(quarters * piece_rows, width + EXTRA)
    text = block[:, :width]
    if own:
        images = own_images[0]
        logits = scale * dot(text, images, (1, 1)) + bias
        same = text_docs[0] == image_docs[0]
        sign = jnp.where(same, 1.0, -1.0)
        loss, weight = loss_and_weight(-sign * logits)
        own_loss[0] = jnp.sum(loss, axis=0, keepdims=True)
        acc[...] = dot((-sign * weight).astype(BF16), images, (1, 0))
    else:
        acc[...] = jnp.zeros_like(acc)

    @pl.when(t == 0)
    def _():
        for copy in copies:
            copy.wait()

    add_tiles(t, text, acc, sources, slots, counts, scale_bias, arrived, pair_loss)
    inverse = jnp.sum(block[:, width:].astype(F32), axis=-1, keepdims=True)
    unit = text.astype(F32)
    grad = scale * acc[...]
    along = jnp.sum(unit * grad, axis=-1, keepdims=True)
    acc[...] = (grad - unit * along) * inverse
    for k in range(quarters):
        start = pl.multiple_of(lax.rem(place[0] + k, quarters) * part, part)
        values = acc[:, pl.ds(start, part)].astype(BF16)
        for j in range(quarters):
            chunks[k, j, 0] = values[j * piece_rows : (j + 1) * piece_rows]


def pick_kernel(table, place, from_ref, *refs, step, sizes, onward, carries):
    z_size, y_size, c_size = sizes
    sems = refs[-1]
    outs = y_size + (onward > 0) + carries
    to_refs = refs[-1 - outs : -1]
    count = from_ref.shape[0]
    back = jnp.where(place[2] == 0, step, z_size - step)
    z = lax.rem(place[3] - back + z_size, z_size)
    copies = []
    if onward:
        copies.append(pltpu.make_async_copy(from_ref.at[pl.ds(0, onward)], to_refs[y_size], sems.at[0]))
    if carries:
        copies.append(pltpu.make_async_copy(refs[0], to_refs[-1], sems.at[1]))
    for dy in range(y_size):
        y = lax.rem(place[1] + dy, y_size)
        for to in range(c_size):
            for j in range(count):
                source = z * c_size + lax.rem(place[2] + j, c_size)
                block = table[source, y * c_size + lax.rem(place[2] + to, c_size)]
                n = to * count + j
                sem = sems.at[2 + dy * c_size * count + n]
                copies.append(pltpu.make_async_copy(from_ref.at[j, block], to_refs[dy].at[n], sem))
    for copy in copies:
        copy.start()
    for copy in copies:
        copy.wait()


def head_kernel(place, grad_0, grad_1, grad_2, grad_3, feats, first_done, keep, give, turned, *, sizes, strip):
    z_part, y_size, c_size = sizes

    @pl.when(pl.program_id(0) == 0)
    def _():
        total = sum(g[...].astype(F32) for g in (grad_0, grad_1, grad_2, grad_3))
        flipped = total.T.astype(BF16)
        for zz in range(z_part):
            for y in range(y_size):
                for c in range(c_size):
                    block = flipped[((zz * y_size + y) * c_size + c) * strip :][:strip]
                    y_rel = lax.rem(y - place[1] + y_size, y_size)
                    c_rel = lax.rem(c - place[2] + c_size, c_size)
                    to = ((c_rel * y_size + y_rel) * z_part + zz) * strip
                    turned[pl.ds(pl.multiple_of(to, strip), strip)] = block

    half = keep.shape[0]
    total = dot(turned[...], feats[...], (1, 0)).astype(BF16)
    keep[...] = total[:half]
    give[...] = total[half:]


def whole(memory=pltpu.VMEM):
    return pl.BlockSpec(memory_space=memory)


def on_device(
    text_features, head_weight, image_embeds, doc_ids, hard_lists, logit_scale, logit_bias
):
    z_size, y_size, c_size, x_size = (lax.axis_size(name) for name in ("z", "y", "c", "x"))
    z, y, c, x = (lax.axis_index(name) for name in ("z", "y", "c", "x"))
    dp_count = z_size * y_size * c_size
    dp_index = (z * y_size + y) * c_size + c
    blocks, _, piece_rows, feat_width = text_features.shape
    block_rows = image_embeds.shape[1]
    emb_width = head_weight.shape[1]
    rows = blocks * piece_rows
    part = emb_width // x_size
    strip = emb_width // dp_count
    block_iota = jnp.arange(blocks, dtype=jnp.int32)
    peer_iota = jnp.arange(dp_count, dtype=jnp.int32)
    place = jnp.stack([x, y, c, z]).astype(jnp.int32)
    features = text_features.reshape(rows, feat_width)

    owners = jnp.where(hard_lists >= 0, hard_lists // blocks, -1).reshape(dp_count, blocks, -1)
    line = owners.reshape(z_size, y_size, c_size, blocks, -1)
    line = lax.dynamic_index_in_dim(line, y, 1, keepdims=False).reshape(z_size * c_size, blocks, -1)
    plane = z * y_size * c_size + jnp.arange(y_size * c_size, dtype=jnp.int32)
    wanted = jnp.any(line[:, None] == plane[:, None, None], axis=3)
    table = jnp.sum(wanted.astype(jnp.int32) * block_iota, axis=2)

    own_images = lax.dynamic_slice_in_dim(image_embeds, x * piece_rows, piece_rows, 1)
    own_images = unit_rows(own_images.astype(F32))[0].astype(BF16)
    tile = min(1024, feat_width)
    project = pl.pallas_call(
        project_kernel,
        grid=(feat_width // tile,),
        out_shape=jax.ShapeDtypeStruct((x_size, rows, emb_width + EXTRA), BF16),
        in_specs=[
            pl.BlockSpec((rows, tile), lambda i: (0, i)),
            pl.BlockSpec((tile, emb_width), lambda i: (i, 0)),
        ]
        + [whole(pl.ANY)] * 2,
        out_specs=pl.BlockSpec((x_size, rows, emb_width + EXTRA), lambda i: (0, 0, 0)),
        scratch_shapes=[pltpu.VMEM((rows, emb_width), F32)],
        compiler_params=pltpu.CompilerParams(vmem_limit_bytes=60 << 20),
        cost_estimate=pl.CostEstimate(flops=1, bytes_accessed=1, transcendentals=0),
        name="project",
    )
    groups, texts, sent_features = exchange_images(
        own_images,
        table,
        place,
        (z_size, y_size, c_size),
        lambda *first: project(features, head_weight, *first),
        features,
    )
    feats = lax.all_gather(sent_features, "x", axis=0, tiled=False)

    arrays, starts, slot_base, turns = [], [], [], 0
    for group in groups:
        count = group[0].shape[0] // c_size
        slot_base.append(turns)
        for array in group:
            arrays.append(array)
            starts.append(turns)
            turns += count
    away = jnp.where(c == 0, z - peer_iota // (y_size * c_size), peer_iota // (y_size * c_size) - z) % z_size
    over_y = (y - peer_iota // c_size) % y_size
    over_c = (c - peer_iota) % c_size
    ends = (away == 0) | (away == z_size // 2)
    have = jnp.where(ends, over_c == 0, away < z_size // 2)
    base = sum(jnp.where(away == k, b, 0) for k, b in enumerate(slot_base))
    slot_of = base + jnp.where(ends, over_y, over_y * c_size + over_c)

    text_docs = doc_ids.reshape(blocks, block_rows, 1)
    image_docs = lax.dynamic_slice_in_dim(doc_ids, x * piece_rows, piece_rows, 1)[:, None]
    scale_bias = jnp.stack([logit_scale, logit_bias])

    def lists(holder, here):
        hit = owners == holder
        which = jnp.sum(hit * (hard_lists % blocks).reshape(owners.shape), axis=(1, 2))
        mine = (jnp.any(hit, axis=(1, 2)) & here)[None] & (which[None] == block_iota[:, None])
        before = peer_iota[None] < peer_iota[:, None]
        order = jnp.sum((mine[:, None] & before).astype(jnp.int32), axis=2)
        at = mine[:, None] & (order[:, None] == peer_iota[:, None])
        sources = jnp.sum(jnp.where(at, peer_iota, 0), axis=2)
        return sources, jnp.sum(jnp.where(at, slot_of, 0), axis=2), jnp.sum(mine.astype(jnp.int32), axis=1)

    loss_shape = jax.ShapeDtypeStruct((dp_count, 1, piece_rows), F32)

    def pairs(holder, pieces, own):
        extra, extra_specs, losses, loss_specs = [], [], [], []
        if own:
            extra = [own_images, image_docs, text_docs]
            extra_specs = [pl.BlockSpec((1,) + v.shape[1:], lambda t: (t, 0, 0)) for v in extra]
            losses = [jax.ShapeDtypeStruct((blocks, 1, piece_rows), F32)]
            loss_specs = [pl.BlockSpec((1, 1, piece_rows), lambda t: (t, 0, 0))]
        return pl.pallas_call(
            functools.partial(pair_kernel, starts=starts, own=own),
            grid=(blocks,),
            out_shape=[
                jax.ShapeDtypeStruct((x_size, x_size, blocks, piece_rows, part), BF16),
                loss_shape,
            ]
            + losses,
            in_specs=[whole(pltpu.SMEM)] * 5
            + [pl.BlockSpec((x_size, 1, piece_rows, emb_width + EXTRA), lambda t: (0, t, 0, 0))]
            + extra_specs
            + [whole(pl.ANY)] * len(arrays),
            out_specs=[
                pl.BlockSpec((x_size, x_size, 1, piece_rows, part), lambda t: (0, 0, t, 0, 0)),
                pl.BlockSpec(loss_shape.shape, lambda t: (0, 0, 0)),
            ]
            + loss_specs,
            scratch_shapes=[
                pltpu.VMEM((block_rows, emb_width), F32),
                pltpu.VMEM((turns, piece_rows, emb_width), BF16),
                pltpu.SemaphoreType.DMA((len(arrays),)),
            ],
            compiler_params=pltpu.CompilerParams(vmem_limit_bytes=60 << 20),
            cost_estimate=pl.CostEstimate(flops=1, bytes_accessed=1, transcendentals=0),
            name="pairs",
        )(
            *lists(holder, have),
            place,
            scale_bias,
            pieces.reshape(x_size, blocks, piece_rows, emb_width + EXTRA),
            *extra,
            *arrays,
        )

    other_texts = lax.ppermute(texts, "c", shifted(c_size, 1))
    other_chunks, other_loss = pairs(dp_index + 1 - 2 * c, other_texts, False)
    chunks, pair_loss, own_loss = pairs(dp_index, texts, True)

    returned = lax.all_to_all(
        jnp.concatenate([pair_loss, other_loss], axis=1), DP, split_axis=0, concat_axis=0, tiled=True
    )

    taken = lax.ppermute(other_chunks, "c", shifted(c_size, 1))
    grads = []
    for k in range(x_size):
        total = (chunks[k].astype(F32) + taken[k].astype(F32)).astype(BF16).reshape(x_size * rows, part)
        grads.append(lax.ppermute(total, "x", shifted(x_size, k)) if k else total)
    z_part = z_size // x_size
    half = part // c_size
    keep, give = pl.pallas_call(
        functools.partial(head_kernel, sizes=(z_part, y_size, c_size), strip=strip),
        grid=(feat_width // tile,),
        out_shape=(
            jax.ShapeDtypeStruct((half, feat_width), BF16),
            jax.ShapeDtypeStruct((half, feat_width), BF16),
        ),
        in_specs=[whole(pltpu.SMEM)]
        + [whole()] * 4
        + [pl.BlockSpec((x_size * rows, tile), lambda i: (0, i)), whole(pl.ANY)],
        out_specs=(
            pl.BlockSpec((half, tile), lambda i: (0, i)),
            pl.BlockSpec((half, tile), lambda i: (0, i)),
        ),
        scratch_shapes=[pltpu.VMEM((part, x_size * rows), BF16)],
        compiler_params=pltpu.CompilerParams(vmem_limit_bytes=60 << 20),
        cost_estimate=pl.CostEstimate(
            flops=2 * rows * feat_width * emb_width, bytes_accessed=16 << 20, transcendentals=0
        ),
        name="head",
    )(place, *grads, feats.reshape(x_size * rows, feat_width), returned)

    swapped = returned.reshape(-1, c_size, 2, piece_rows)[:, ::-1, 1].reshape(dp_count, piece_rows)
    returned = returned[:, 0] + swapped
    my_owners = lax.dynamic_index_in_dim(owners, dp_index, 0, keepdims=False)
    asked = jnp.any(my_owners[None] == peer_iota[:, None, None], axis=2)
    remote_loss = jnp.sum(jnp.where(asked[..., None], returned[:, None], 0.0), axis=0)
    row_loss = (own_loss.reshape(blocks, piece_rows) + remote_loss) / block_rows
    return (row_loss, add_over_dp(keep, give, (z_size, y_size, c_size, x_size), z, strip))


def add_over_dp(keep, give, sizes, z, strip):
    z_size, y_size, c_size, x_size = sizes
    z_part = z_size // x_size
    width = keep.shape[1]

    def add(*values):
        return sum(v.astype(F32) for v in values).astype(BF16)

    total = add(keep, lax.ppermute(give, "c", shifted(c_size, 1)))
    total = total.reshape(y_size, z_part * strip, width)
    total = add(
        total[0], *(lax.ppermute(total[k], "y", shifted(y_size, k)) for k in range(1, y_size))
    ).reshape(z_part, strip, width)
    low, top = z % 2, z // (z_size // 2)
    given = lax.dynamic_index_in_dim(total, 1 - low, 0, keepdims=False)
    kept = lax.dynamic_index_in_dim(total, low, 0, keepdims=False)
    total = add(kept, lax.ppermute(given, "z", [(i, i ^ 1) for i in range(z_size)]))
    total = total.reshape(strip, 2, width // 2)
    given = lax.dynamic_index_in_dim(total, 1 - top, 1, keepdims=False)
    kept = lax.dynamic_index_in_dim(total, top, 1, keepdims=False)
    total = add(kept, lax.ppermute(given, "z", [(i, (i + z_size // 2) % z_size) for i in range(z_size)]))
    total = total.reshape(strip, 2, width // 4)
    final = 0.0
    for flip in range(2):
        pairs = []
        for z_from in range(z_size):
            bit = (z_from // 2 % 2) ^ flip
            for x_from in range(x_size):
                to_z, to_x = z_part * x_from + z_from % 2, z_from // (z_size // 2) * 2 + bit
                pairs.append((z_from * x_size + x_from, to_z * x_size + to_x))
        chunk = lax.dynamic_index_in_dim(total, (z // 2 % 2) ^ flip, 1, keepdims=False)
        final = final + lax.ppermute(chunk, ("z", "x"), pairs).astype(F32)
    return final.T


def exchange_images(own_images, table, place, sizes, project, features):
    z_size, y_size, c_size = sizes
    onward = []
    for z in range(z_size):
        onward.append((z * c_size, (z + 1) % z_size * c_size))
        onward.append((z * c_size + 1, (z - 1) % z_size * c_size + 1))
    moving = jnp.stack([own_images, lax.ppermute(own_images, "c", shifted(c_size, 1))])
    groups = []
    last = z_size // 2
    for step in range(last + 1):
        here = own_images[None] if step == 0 else lax.ppermute(moving, ("z", "c"), onward)
        keeps = 0 if step in (0, last) else 1 if step == last - 1 else c_size
        shape = (c_size * here.shape[0],) + own_images.shape[1:]
        outs = [jax.ShapeDtypeStruct(shape, BF16)] * y_size
        if keeps:
            outs.append(jax.ShapeDtypeStruct((keeps,) + own_images.shape, BF16))
        before = [groups[step - 1][1], groups[step - 1][-1]] if step in (1, 2, last) else []
        if step == 2:
            before.append(groups[0][y_size // 2])
        if step == last:
            before += [groups[k][y_size // 2] for k in range(1, last - 1)] + groups[last - 2][1:]
        if step == 1:
            text_emb = project(here, picked[0])
            texts = lax.all_to_all(text_emb, "x", split_axis=0, concat_axis=0, tiled=True)
        elif step == 2:
            before.append(text_emb)
        carried = [features] if step == 2 else [texts] if step == last else []
        if carried:
            outs.append(jax.ShapeDtypeStruct(carried[0].shape, carried[0].dtype))
        picked = pl.pallas_call(
            functools.partial(pick_kernel, step=step, sizes=sizes, onward=keeps, carries=len(carried)),
            out_shape=outs,
            in_specs=[whole(pltpu.SMEM)] * 2 + [whole()] * (1 + len(carried)) + [whole(pl.ANY)] * len(before),
            out_specs=[whole(pl.ANY)] * len(outs),
            scratch_shapes=[pltpu.SemaphoreType.DMA((2 + y_size * shape[0],))],
            cost_estimate=pl.CostEstimate(flops=1, bytes_accessed=1, transcendentals=0),
            name="pick",
        )(table, place, here, *carried, *before)
        if keeps:
            moving = picked[y_size]
        if step == 2:
            features = picked[-1]
        if step == last:
            texts = picked[-1]
        groups.append(
            [picked[0]] + [lax.ppermute(picked[n], "y", shifted(y_size, n)) for n in range(1, y_size)]
        )
    return groups, texts, features


def solution(mesh):
    x_size = mesh.shape["replica"]
    c_size = 2
    z_size = 2 * x_size
    y_size = mesh.shape["dp"] // (z_size * c_size)
    fine = Mesh(mesh.devices.reshape(z_size, y_size, c_size, x_size), ("z", "y", "c", "x"))
    placed = (P(DP, "x", None, None), P(), P(DP, None, None), P(DP, None), P(), P(), P())
    return jax.shard_map(
        on_device,
        mesh=fine,
        in_specs=placed,
        out_specs=(P(DP, "x"), P("x", DP)),
        check_vma=False,
    )
```
